32 devices in a mesh: req: 16 (over z, y, x), mp: 2 (over core).
Axes of the slice: x: 2, y: 2, z: 4, core: 2. Of those that a mesh axis runs over, the one named last changes fastest.
Arguments:
- queries: bfloat16 [4096, 2048], P('req', 'mp')
- keys: bfloat16 [4096, 1024], P('req', 'mp'), may hold values from -6 to 6
- values: bfloat16 [4096, 1024], P('req', 'mp'), may hold values from -6 to 6
- out_weight: bfloat16 [2048, 4608], P(None, 'mp'), may hold values from -0.125 to 0.125
- out_grad: bfloat16 [4096, 4608], P('req', 'mp'), may hold values from -6 to 6
- bank: float32 [4096, 2, 1024], P('req', None, 'mp'), may hold values from -6 to 6
- moment_one: float32 [4096, 2, 1024], P('req', None, 'mp')
- moment_two: float32 [4096, 2, 1024], P('req', None, 'mp'), as said below
- block_list: int32 [16, 8], replicated, may hold values from 0 to 31, as said below
- block_count: int32 [16], replicated, may hold values from 4 to 8, as said below
- token_count: int32 [16], P('req'), may hold values from 128 to 256, as said below
Outputs:
- attn_out: float32 [4096, 4608], P('req', 'mp')
- bank_next: float32 [4096, 2, 1024], P('req', None, 'mp')
- moment_next: float32 [4096, 2, 1024], P('req', None, 'mp')
- second_next: float32 [4096, 2, 1024], P('req', None, 'mp')
The draws below stay inside these ranges and needn't reach their ends.
Inputs may be any that keep to these rules, and one draw needn't show every extreme that they name: `block_list`: the 8 blocks of one request have distinct owners (block b belongs to owner b // 2). `block_count`: some request uses all 8 entries. The live tokens of a request are its first token_count[r] rows; some request fills all 256. `moment_two`: positive.
All inputs are finite; a program needn't handle non-finite values.
Results may differ from the reference program's by a relative error of at most 0.035.
Values may be sent and summed in bfloat16 or wider, within the bound.
No kernel may reach another device: no remote copies, remote signals or barrier semaphores. Data moves between devices by JAX's collectives and lax.ppermute only.
A program may use at most 128 MiB of HBM per device.

```python
import math
import jax
import jax.numpy as jnp
from jax import lax

D = 4608
HEADS = 16
KV_HEADS = 8
HD = 128
BLOCK = 128
BLK_DEV = 2
TOK_DEV = 256
REQS = 16
TOKENS = 4096
BLOCKS = 32
VECTORS = 4096
MAXB = 8


def draw_queries(key, part):
    shape = (TOKENS, HEADS * HD)
    base_key, boost_key, offset_key = jax.random.split(jax.random.fold_in(key, 51), 3)
    period = max(TOK_DEV // 8, 2)
    position = jnp.arange(TOKENS, dtype=jnp.int32) % TOK_DEV
    offset = jnp.repeat(jax.random.randint(offset_key, (REQS,), 0, period), TOK_DEV)
    picked = position % period == offset
    boost = jax.random.uniform(boost_key, (TOKENS,), jnp.float32, 6.0, 12.0)
    base = jnp.clip(jax.random.normal(base_key, shape, jnp.float32), -6.0, 6.0)
    row_scale = jnp.ones((TOKENS,), jnp.float32)
    factor = jnp.where(picked, boost, row_scale)
    return (base * factor[:, None]).astype(jnp.bfloat16)


def draw_block_list(key, part):
    owner_total = BLOCKS // BLK_DEV
    score_key, pick_key = jax.random.split(jax.random.fold_in(key, 11))
    scores = jax.random.randint(score_key, (REQS, owner_total), 0, 1 << 20) * owner_total
    scores = scores + jnp.arange(owner_total, dtype=jnp.int32)[None, :]
    order = jnp.argsort(scores, axis=1, stable=True)[:, :MAXB].astype(jnp.int32)
    pick = jax.random.randint(pick_key, (REQS, MAXB), 0, BLK_DEV)
    return (order * BLK_DEV + pick).astype(jnp.int32)


def draw_block_count(key, part):
    least = MAXB * 3 // 5
    count_key, place_key = jax.random.split(jax.random.fold_in(key, 23))
    counts = jax.random.randint(count_key, (REQS,), least, MAXB + 1)
    place = jax.random.randint(place_key, (), 0, REQS)
    counts = counts.at[place].set(MAXB)
    counts = counts.at[(place + 1) % REQS].set(least)
    return counts.astype(jnp.int32)


def draw_token_count(key, part):
    least = TOK_DEV // 2
    count_key, place_key = jax.random.split(jax.random.fold_in(key, 37))
    counts = jax.random.randint(count_key, (REQS,), least, TOK_DEV + 1)
    place = jax.random.randint(place_key, (), 0, REQS)
    counts = counts.at[place].set(TOK_DEV)
    counts = counts.at[(place + 1) % REQS].set(least)
    return counts.astype(jnp.int32)


def gradient_scale():
    return 1.5 * math.sqrt(0.15 * BLOCKS * TOK_DEV) / (0.8 * MAXB * BLOCK + 0.5 * TOK_DEV)


def draw_moment_one(key, part):
    shape = (VECTORS, 2, KV_HEADS * HD)
    base = jax.random.normal(key, shape, jnp.float32)
    return base * gradient_scale()


def draw_moment_two(key, part):
    shape = (VECTORS, 2, KV_HEADS * HD)
    ratio = jnp.exp(jax.random.uniform(key, shape, jnp.float32, math.log(0.001), math.log(0.1)))
    return ratio * gradient_scale() * gradient_scale()


def shard_levels(key, dims, cuts, low, top_value):
    loudness, own = 1.0, jax.random.fold_in(key, 6)
    for dim, shards_of in cuts:
        steps = jnp.exp(jax.random.uniform(jax.random.fold_in(own, dim), (shards_of,), jnp.float32, low / len(cuts), top_value / len(cuts)))
        loudness = loudness * jnp.repeat(steps, dims[dim] // shards_of).reshape([-1 if axis == dim else 1 for axis in range(len(dims))])
    return loudness


def gaussian(stream_key, shape, scale, limit, pieces=(), kind=jnp.bfloat16):
    result = scale * jax.random.normal(stream_key, shape, jnp.float32)
    if pieces:
        result = result * shard_levels(stream_key, shape, pieces, -0.22, 0.18)
    return jnp.clip(result, -limit, limit).astype(kind)


def setup_inputs(seed: int = 0) -> dict:
    seeds = jax.random.split(jax.random.key(seed), 12)
    queries = draw_queries(jax.random.fold_in(seeds[11], 71), 0)
    keys = gaussian(seeds[1], (TOKENS, KV_HEADS * HD), 1.0, 6.0, ((0, 16), (1, 2)))
    values = gaussian(seeds[2], (TOKENS, KV_HEADS * HD), 1.0, 6.0, ((0, 16), (1, 2)))
    out_weight = gaussian(seeds[3], (HEADS * HD, D), (HEADS * HD) ** -0.5, 0.125, ((1, 2),))
    out_grad = gaussian(seeds[4], (TOKENS, D), 1.0, 6.0, ((0, 16), (1, 2)))
    bank = gaussian(seeds[5], (VECTORS, 2, KV_HEADS * HD), 1.0, 6.0, ((0, 16), (2, 2)), jnp.float32)
    moment_one = draw_moment_one(jax.random.fold_in(seeds[11], 71), 0)
    moment_two = draw_moment_two(jax.random.fold_in(seeds[11], 71), 0)
    block_list = draw_block_list(jax.random.fold_in(seeds[11], 71), 0)
    block_count = draw_block_count(jax.random.fold_in(seeds[11], 71), 0)
    token_count = draw_token_count(jax.random.fold_in(seeds[11], 71), 0)
    return dict(queries=queries, keys=keys, values=values, out_weight=out_weight, out_grad=out_grad, bank=bank, moment_one=moment_one, moment_two=moment_two, block_list=block_list, block_count=block_count, token_count=token_count)


softcap = 50.0
qscale = 1.0 / 12.0
beta_one = 0.9
beta_two = 0.999
learn_rate = 0.3
adam_eps = 1e-08
bias_one = 1.0 - 0.9 ** 10
bias_two = 1.0 - 0.999 ** 10

def capped(raw):
    return softcap * jnp.tanh(raw / softcap)

def rounded(value):
    return lax.optimization_barrier(value.astype(jnp.bfloat16)).astype(jnp.float32)

def reference(queries, keys, values, out_weight, out_grad, bank, moment_one, moment_two, block_list, block_count, token_count):
    group = HEADS // KV_HEADS
    bank_half = bank.astype(jnp.bfloat16).reshape(BLOCKS, BLOCK, 2, KV_HEADS * HD)
    position = jnp.arange(TOK_DEV, dtype=jnp.int32)
    causal = position[:, None] >= position[None, :]
    slot_block = jnp.arange(MAXB * BLOCK, dtype=jnp.int32) // BLOCK

    def request_step(grad_total, inputs):
        query_rows, key_rows, value_rows, grad_rows, listed, used_blocks, used_tokens = inputs
        query_four = query_rows.reshape(TOK_DEV, KV_HEADS, group, HD).astype(jnp.float32)
        key_three = key_rows.reshape(TOK_DEV, KV_HEADS, HD).astype(jnp.float32)
        value_three = value_rows.reshape(TOK_DEV, KV_HEADS, HD).astype(jnp.float32)
        prefix = bank_half[listed]
        prefix_keys = prefix[:, :, 0].reshape(MAXB * BLOCK, KV_HEADS, HD).astype(jnp.float32)
        prefix_values = prefix[:, :, 1].reshape(MAXB * BLOCK, KV_HEADS, HD).astype(jnp.float32)
        slot_ok = slot_block < used_blocks
        prefix_capped = capped(jnp.einsum('tkgd,skd->kgts', query_four, prefix_keys) * qscale)
        prefix_exp = jnp.where(slot_ok, jnp.exp(prefix_capped), 0.0)
        token_capped = capped(jnp.einsum('tkgd,skd->kgts', query_four, key_three) * qscale)
        token_exp = jnp.where(causal, jnp.exp(token_capped), 0.0)
        denominator = lax.optimization_barrier(jnp.sum(prefix_exp, axis=-1)) + lax.optimization_barrier(jnp.sum(token_exp, axis=-1))
        prefix_prob = prefix_exp / denominator[..., None]
        prefix_weights = rounded(prefix_prob)
        token_weights = rounded(token_exp / denominator[..., None])
        mixed = jnp.einsum('kgts,skd->tkgd', prefix_weights, prefix_values) + jnp.einsum('kgts,skd->tkgd', token_weights, value_three)
        row_ok = position[:, None] < used_tokens
        heads_out = jnp.where(row_ok, mixed.reshape(TOK_DEV, HEADS * HD), 0.0).astype(jnp.bfloat16)
        out_rows = jnp.dot(heads_out, out_weight, preferred_element_type=jnp.float32)
        head_grad = jnp.dot(grad_rows, out_weight.T, preferred_element_type=jnp.float32)
        grad_heads = rounded(jnp.where(row_ok, head_grad, 0.0)).reshape(TOK_DEV, KV_HEADS, group, HD)
        heads_four = heads_out.astype(jnp.float32).reshape(TOK_DEV, KV_HEADS, group, HD)
        delta = jnp.einsum('tkgd,tkgd->kgt', grad_heads, heads_four)
        dprob = jnp.einsum('tkgd,skd->kgts', grad_heads, prefix_values)
        dscore = rounded(prefix_prob * (dprob - delta[..., None]) * (1.0 - (prefix_capped / softcap) ** 2) * qscale)
        key_grad = jnp.einsum('kgts,tkgd->skd', dscore, query_four)
        value_grad = jnp.einsum('kgts,tkgd->skd', prefix_weights, grad_heads)
        block_grad = jnp.stack((key_grad.reshape(MAXB, BLOCK, KV_HEADS * HD), value_grad.reshape(MAXB, BLOCK, KV_HEADS * HD)), axis=2)
        return (grad_total.at[listed].add(block_grad), out_rows)
    inputs = (queries.reshape(REQS, TOK_DEV, HEADS * HD), keys.reshape(REQS, TOK_DEV, KV_HEADS * HD), values.reshape(REQS, TOK_DEV, KV_HEADS * HD), out_grad.reshape(REQS, TOK_DEV, D), block_list, block_count, token_count)
    start_grad = jnp.zeros((BLOCKS, BLOCK, 2, KV_HEADS * HD), jnp.float32)
    grad_total, out_rows = lax.scan(request_step, start_grad, inputs)
    attn_out = out_rows.reshape(REQS * TOK_DEV, D)
    grad = grad_total.reshape(VECTORS, 2, KV_HEADS * HD)
    moment_next = beta_one * moment_one + (1.0 - beta_one) * grad
    second_next = beta_two * moment_two + (1.0 - beta_two) * grad * grad
    bank_next = bank - learn_rate * (moment_next / bias_one) / (jnp.sqrt(second_next / bias_two) + adam_eps)
    return (attn_out, bank_next, moment_next, second_next)
```

```python
import functools

import jax
import jax.numpy as jnp
from jax import lax
from jax.experimental import pallas as pl
from jax.experimental.pallas import tpu as pltpu
from jax.sharding import PartitionSpec as P

HD = 128
BLOCK = 128

softcap = 50.0
qscale = 1.0 / 12.0
beta_one = 0.9
beta_two = 0.999
learn_rate = 0.3
adam_eps = 1e-08
bias_one = 1.0 - 0.9**10
bias_two = 1.0 - 0.999**10

f32 = jnp.float32
bf16 = jnp.bfloat16
MIB = 1 << 20


def nn(a, b):
    return lax.dot_general(a, b, (((1,), (0,)), ((), ())), preferred_element_type=f32)


def call(body, out, grid_spec=None, limit=32, cost=None, **more):
    return pl.pallas_call(
        body,
        out_shape=out,
        compiler_params=pltpu.CompilerParams(vmem_limit_bytes=limit * MIB),
        cost_estimate=cost,
        **({"grid_spec": grid_spec} if grid_spec is not None else {}),
        **more,
    )


def cost(flops, nbytes, trans=0):
    return pl.CostEstimate(flops=flops, bytes_accessed=nbytes, transcendentals=trans)


def split_body(parts, copies, bank_ref, out_ref):
    rows = out_ref.shape[1]
    for part in range(parts):
        chunk = bank_ref[pl.ds(part, rows, stride=parts), :].astype(bf16)
        for copy in range(copies):
            out_ref[copy * parts + part] = chunk


def pick_body(parts, slots, meta, lists, counts, all_ref, *outs):
    me = meta[0]
    for k in range(parts):
        row = me ^ k

        def one(s, carry, k=k, row=row):
            outs[k][s] = all_ref[lists[row, s]]
            return carry

        lax.fori_loop(0, slots, one, 0, unroll=4)


def head_body(step, parts, slots, meta, counts, *refs):
    if step:
        refs = refs[1:]
    q_ref, k_ref, v_ref, g_ref, a_ref, b_ref, ho_ref, ga_ref, gb_ref, q_two, t_all, e_all, w_all = refs
    tokens = q_ref.shape[0]
    wide = 2 * tokens
    used = counts[meta[0]]
    live_tokens = meta[1]
    odd = meta[0] & 1
    tile = 2 * BLOCK
    tiles = slots // 2

    lane = lax.broadcasted_iota(jnp.int32, (1, wide), 1)
    token = jnp.where(lane >= tokens, lane - tokens, lane)
    row_ok = token < live_tokens

    q_two[0:tokens, :] = q_ref[:, 0:HD]
    q_two[tokens:wide, :] = q_ref[:, HD : 2 * HD]
    q_t = q_two[...].T
    grad = jnp.concatenate([g_ref[0:HD, :], g_ref[HD : 2 * HD, :]], axis=1)
    grad = jnp.where(row_ok, grad, 0.0).astype(bf16)
    grad_two = grad.T

    def pair(ref_even, ref_odd, i):
        even = ref_even[pl.ds(2 * i, 2)].reshape(tile, HD)
        other = ref_odd[pl.ds(2 * i, 2)].reshape(tile, HD)
        return jnp.where(odd == 0, even, other)

    raw = nn(k_ref[...], q_t)
    row = lax.broadcasted_iota(jnp.int32, (tokens, wide), 0)
    token_exp = jnp.where(row <= token, jnp.exp(softcap * jnp.tanh(raw * (qscale / softcap))), 0.0)
    total = jnp.sum(token_exp, axis=0, keepdims=True)

    def scores(i, total):
        raw = nn(pair(a_ref, b_ref, i), q_t)
        tanh = jnp.tanh(raw * (qscale / softcap))
        slot = 2 * i + lax.broadcasted_iota(jnp.int32, (tile, 1), 0) // BLOCK
        exps = jnp.where(slot < used, jnp.exp(softcap * tanh), 0.0)
        at = pl.ds(i * tile, tile)
        t_all[at, :] = tanh
        e_all[at, :] = exps
        return total + jnp.sum(exps, axis=0, keepdims=True)

    unroll = tiles if tiles <= 4 else 1
    total = lax.fori_loop(0, tiles, scores, total, unroll=unroll)
    inverse = 1.0 / total

    mixed = nn(v_ref[...].T, (token_exp * inverse).astype(bf16))

    def mix(i, mixed):
        at = pl.ds(i * tile, tile)
        weights = (e_all[at, :] * inverse).astype(bf16)
        w_all[at, :] = weights
        return mixed + nn(pair(b_ref, a_ref, i).T, weights)

    mixed = lax.fori_loop(0, tiles, mix, mixed, unroll=unroll)
    out = jnp.where(row_ok, mixed, 0.0).astype(bf16)
    delta = jnp.sum(grad.astype(f32) * out.astype(f32), axis=0, keepdims=True)
    ho_ref[:, 0:HD] = out[:, 0:tokens].T
    ho_ref[:, HD : 2 * HD] = out[:, tokens:wide].T
    scaled = inverse * qscale

    def back(i, carry):
        at = pl.ds(i * tile, tile)
        dprob = nn(pair(b_ref, a_ref, i), grad)
        tanh = t_all[at, :]
        dscore = ((e_all[at, :] * scaled) * (dprob - delta) * (1.0 - tanh * tanh)).astype(bf16)
        dkey = nn(dscore, q_two[...]).astype(bf16).reshape(2, BLOCK, HD)
        dvalue = nn(w_all[at, :], grad_two).astype(bf16).reshape(2, BLOCK, HD)
        ga_ref[pl.ds(2 * i, 2)] = jnp.where(odd == 0, dkey, dvalue)
        gb_ref[pl.ds(2 * i, 2)] = jnp.where(odd == 0, dvalue, dkey)
        return carry

    lax.fori_loop(0, tiles, back, 0, unroll=unroll)


def sum_body(parts, slots, meta, lists, counts, *refs):
    out_ref, total = refs[parts], refs[parts + 1]
    me = meta[0]
    total[...] = jnp.zeros_like(total)
    for k in range(parts):
        row = me ^ k

        def one(s, carry, k=k, row=row):
            at = lists[row, s]
            total[at] += refs[k][s].astype(f32)
            return carry

        lax.fori_loop(0, counts[row], one, 0)
    out_ref[...] = total[...].astype(bf16)


def adam_body(parts, copies, grad_ref, bank_ref, one_ref, two_ref, bank_out, one_out, two_out):
    rows = grad_ref.shape[1]
    for part in range(parts):
        if copies <= 4:
            grad = grad_ref[part].astype(f32)
            for copy in range(1, copies):
                grad = grad + grad_ref[copy * parts + part].astype(f32)
        else:
            grad = lax.fori_loop(
                0,
                copies,
                lambda copy, run, part=part: run + grad_ref[copy * parts + part].astype(f32),
                jnp.zeros((rows, HD), f32),
            )
        at = pl.ds(part, rows, stride=parts)
        moment = beta_one * one_ref[at, :] + (1.0 - beta_one) * grad
        second = beta_two * two_ref[at, :] + (1.0 - beta_two) * grad * grad
        one_out[at, :] = moment
        two_out[at, :] = second
        bank_out[at, :] = bank_ref[at, :] - learn_rate * (moment / bias_one) / (
            jnp.sqrt(second / bias_two) + adam_eps
        )


def local(
    queries,
    keys,
    values,
    out_weight,
    out_grad,
    bank,
    moment_one,
    moment_two,
    block_list,
    block_count,
    token_count,
):
    owners = lax.axis_size("req")
    mp_size = lax.axis_size("mp")
    me = lax.axis_index("req")
    tokens = queries.shape[0]
    kv_local = keys.shape[1] // HD
    features = queries.shape[1]
    parts = 2 * kv_local
    copies = owners // parts
    rows = bank.shape[0]
    blocks = rows // BLOCK
    slots = block_list.shape[1]
    wide = 2 * tokens
    smem = pl.BlockSpec(memory_space=pltpu.SMEM)
    vmem = pl.BlockSpec(memory_space=pltpu.VMEM)

    def lines(array):
        four = array.reshape(rows, 2, kv_local, HD).transpose(0, 2, 1, 3)
        return four.reshape(rows * parts, HD)

    def unlines(array):
        four = array.reshape(rows, kv_local, 2, HD).transpose(0, 2, 1, 3)
        return four.reshape(rows, 2, kv_local * HD)

    meta = jnp.stack([me.astype(jnp.int32), token_count[0]])

    outgoing = call(
        functools.partial(split_body, parts, copies),
        jax.ShapeDtypeStruct((owners, rows, HD), bf16),
        in_specs=[vmem],
        out_specs=vmem,
        name="split",
    )(lines(bank))
    spread = lax.all_to_all(outgoing, "req", split_axis=0, concat_axis=0, tiled=True)

    partial = lax.dot_general(
        out_weight, out_grad, (((1,), (1,)), ((), ())), preferred_element_type=f32
    )
    if mp_size == 2:
        side = lax.axis_index("mp")
        theirs = lax.dynamic_slice_in_dim(partial, (1 - side) * features, features, 0)
        mine = lax.dynamic_slice_in_dim(partial, side * features, features, 0)
        head_grad = mine + lax.ppermute(theirs, "mp", [(0, 1), (1, 0)])
    else:
        head_grad = lax.psum_scatter(partial, "mp", scatter_dimension=0, tiled=True)

    piece = jax.ShapeDtypeStruct((slots, BLOCK, HD), bf16)
    picked = call(
        functools.partial(pick_body, parts, slots),
        [piece] * parts,
        in_specs=[smem, smem, smem, vmem],
        out_specs=[vmem] * parts,
        name="pick",
    )(meta, block_list, block_count, spread.reshape(owners * blocks, BLOCK, HD))

    def swap(array, k):
        return array if k == 0 else lax.ppermute(array, "req", [(i, i ^ k) for i in range(owners)])

    fetched = [swap(picked[k], k) for k in range(parts)]

    heads_out = None
    returned = [None] * parts
    for step in range(kv_local):

        def column(i, meta, counts, step=step):
            return (0, ((meta[0] & (parts - 1)) >> 1) ^ step)

        def line(i, meta, counts, step=step):
            return (((meta[0] & (parts - 1)) >> 1) ^ step, 0)

        def whole(i, meta, counts):
            return (0, 0, 0)

        block_spec = pl.BlockSpec((slots, BLOCK, HD), whole)
        in_specs = [
            pl.BlockSpec((tokens, 2 * HD), column),
            pl.BlockSpec((tokens, HD), column),
            pl.BlockSpec((tokens, HD), column),
            pl.BlockSpec((2 * HD, tokens), line),
            block_spec,
            block_spec,
        ]
        operands = [queries, keys, values, head_grad, fetched[2 * step], fetched[2 * step + 1]]
        aliases = {}
        if step:
            in_specs = [pl.BlockSpec(memory_space=pl.ANY)] + in_specs
            operands = [heads_out] + operands
            aliases = {2: 0}
        span = slots * BLOCK
        heads_out, returned[2 * step], returned[2 * step + 1] = call(
            functools.partial(head_body, step, parts, slots),
            [jax.ShapeDtypeStruct((tokens, features), bf16), piece, piece],
            grid_spec=pltpu.PrefetchScalarGridSpec(
                num_scalar_prefetch=2,
                grid=(1,),
                in_specs=in_specs,
                out_specs=[pl.BlockSpec((tokens, 2 * HD), column), block_spec, block_spec],
                scratch_shapes=[
                    pltpu.VMEM((wide, HD), bf16),
                    pltpu.VMEM((span, wide), f32),
                    pltpu.VMEM((span, wide), f32),
                    pltpu.VMEM((span, wide), bf16),
                ],
            ),
            limit=48,
            cost=cost(10 * span * wide * HD, 8 * span * HD, 2 * span * wide),
            input_output_aliases=aliases,
            name="head",
        )(meta, block_count, *operands)
    back = [swap(returned[k], k) for k in range(parts)]

    sums = call(
        functools.partial(sum_body, parts, slots),
        jax.ShapeDtypeStruct((owners * blocks, BLOCK, HD), bf16),
        in_specs=[smem] * 3 + [vmem] * parts,
        out_specs=vmem,
        scratch_shapes=[pltpu.VMEM((owners * blocks, BLOCK, HD), f32)],
        name="sums",
    )(meta, block_list, block_count, *back)
    grads = lax.all_to_all(
        sums.reshape(owners, rows, HD), "req", split_axis=0, concat_axis=0, tiled=True
    )

    if mp_size == 2:
        other = lax.ppermute(heads_out, "mp", [(0, 1), (1, 0)])
        both = jnp.concatenate(
            [jnp.where(side == 0, heads_out, other), jnp.where(side == 0, other, heads_out)], axis=1
        )
    else:
        both = lax.all_gather(heads_out, "mp", axis=1, tiled=True)
    attn_out = jnp.dot(both, out_weight, preferred_element_type=f32)

    cut = 4
    state = pl.BlockSpec((rows // cut * parts, HD), lambda i: (i, 0))
    state_out = jax.ShapeDtypeStruct((rows * parts, HD), f32)
    bank_next, moment_next, second_next = call(
        functools.partial(adam_body, parts, copies),
        [state_out] * 3,
        grid=(cut,),
        in_specs=[pl.BlockSpec((owners, rows // cut, HD), lambda i: (0, i, 0))] + [state] * 3,
        out_specs=[state] * 3,
        name="adam",
    )(grads, lines(bank), lines(moment_one), lines(moment_two))
    return (attn_out, unlines(bank_next), unlines(moment_next), unlines(second_next))


def solution(mesh):
    return jax.shard_map(
        local,
        mesh=mesh,
        in_specs=(
            P("req", "mp"),
            P("req", "mp"),
            P("req", "mp"),
            P(None, "mp"),
            P("req", "mp"),
            P("req", None, "mp"),
            P("req", None, "mp"),
            P("req", None, "mp"),
            P(),
            P(),
            P("req"),
        ),
        out_specs=(
            P("req", "mp"),
            P("req", None, "mp"),
            P("req", None, "mp"),
            P("req", None, "mp"),
        ),
        check_vma=False,
    )
```

```python
import functools

import jax
import jax.numpy as jnp
from jax import lax
from jax.experimental import pallas as pl
from jax.experimental.pallas import tpu as pltpu
from jax.sharding import PartitionSpec as P

HD = 128
BLOCK = 128

softcap = 50.0
qscale = 1.0 / 12.0
beta_one = 0.9
beta_two = 0.999
learn_rate = 0.3
adam_eps = 1e-08
bias_one = 1.0 - 0.9**10
bias_two = 1.0 - 0.999**10

f32 = jnp.float32
bf16 = jnp.bfloat16
MIB = 1 << 20


def nn(a, b):
    return lax.dot_general(a, b, (((1,), (0,)), ((), ())), preferred_element_type=f32)


def call(body, out, limit, cost=None, **more):
    return pl.pallas_call(
        body,
        out_shape=out,
        compiler_params=pltpu.CompilerParams(vmem_limit_bytes=limit * MIB),
        cost_estimate=cost,
        **more,
    )


def turned(label):
    return (label << 1) % 8 + label // 4


def offset(label, turn):
    return jnp.where(turn == 1, turned(label), label)


def split_body(parts, copies, turns, bank_ref, out_ref):
    rows = out_ref.shape[1]
    turn = lax.axis_index("mp") if turns else 0
    for part in range(parts):
        line = part % (parts // 2) * 2 + part // (parts // 2)
        chunk = bank_ref[pl.ds(line, rows, stride=parts), :].astype(bf16)
        for copy in range(copies):
            out_ref[copy * parts + offset(part, turn)] = chunk


def pick_body(which, slots, meta, lists, _, all_ref, *outs):
    me = meta[0]
    for out, k in zip(outs, which):
        row = me ^ offset(k, meta[2])

        def one(s, carry, out=out, row=row):
            out[s] = all_ref[lists[row, s]]
            return carry

        lax.fori_loop(0, slots, one, 0, unroll=4)


def head_body(extra, parts, slots, meta, counts, *refs):
    refs = refs[extra:]
    q_ref, k_ref, v_ref, g_ref, a_ref, b_ref, ho_ref, ga_ref, gb_ref, q_two, t_all, e_all, w_all = refs
    tokens = q_ref.shape[0]
    wide = 2 * tokens
    used = counts[meta[0]]
    live_tokens = meta[1]
    odd = meta[3] // (parts // 2)
    tile = 2 * BLOCK
    tiles = slots // 2

    lane = lax.broadcasted_iota(jnp.int32, (1, wide), 1)
    token = jnp.where(lane >= tokens, lane - tokens, lane)
    row_ok = token < live_tokens

    q_two[0:tokens, :] = q_ref[:, 0:HD]
    q_two[tokens:wide, :] = q_ref[:, HD : 2 * HD]
    q_t = q_two[...].T
    grad = jnp.concatenate([g_ref[0:HD, :], g_ref[HD : 2 * HD, :]], axis=1)
    grad = jnp.where(row_ok, grad, 0.0).astype(bf16)
    grad_two = grad.T

    def pair(ref_even, ref_odd, i):
        even = ref_even[pl.ds(2 * i, 2)].reshape(tile, HD)
        other = ref_odd[pl.ds(2 * i, 2)].reshape(tile, HD)
        return jnp.where(odd == 0, even, other)

    raw = nn(k_ref[...], q_t)
    row = lax.broadcasted_iota(jnp.int32, (tokens, wide), 0)
    token_exp = jnp.where(row <= token, jnp.exp(softcap * jnp.tanh(raw * (qscale / softcap))), 0.0)
    total = jnp.sum(token_exp, axis=0, keepdims=True)

    def scores(i, total):
        raw = nn(pair(a_ref, b_ref, i), q_t)
        tanh = jnp.tanh(raw * (qscale / softcap))
        slot = 2 * i + lax.broadcasted_iota(jnp.int32, (tile, 1), 0) // BLOCK
        exps = jnp.where(slot < used, jnp.exp(softcap * tanh), 0.0)
        at = pl.ds(i * tile, tile)
        t_all[at, :] = tanh
        e_all[at, :] = exps
        return total + jnp.sum(exps, axis=0, keepdims=True)

    unroll = tiles if tiles <= 4 else 1
    total = lax.fori_loop(0, tiles, scores, total, unroll=unroll)
    inverse = 1.0 / total

    mixed = nn(v_ref[...].T, (token_exp * inverse).astype(bf16))

    def mix(i, mixed):
        at = pl.ds(i * tile, tile)
        weights = (e_all[at, :] * inverse).astype(bf16)
        w_all[at, :] = weights
        return mixed + nn(pair(b_ref, a_ref, i).T, weights)

    mixed = lax.fori_loop(0, tiles, mix, mixed, unroll=unroll)
    out = jnp.where(row_ok, mixed, 0.0).astype(bf16)
    delta = jnp.sum(grad.astype(f32) * out.astype(f32), axis=0, keepdims=True)
    ho_ref[:, 0:HD] = out[:, 0:tokens].T
    ho_ref[:, HD : 2 * HD] = out[:, tokens:wide].T
    scaled = inverse * qscale

    def back(i, carry):
        at = pl.ds(i * tile, tile)
        dprob = nn(pair(b_ref, a_ref, i), grad)
        tanh = t_all[at, :]
        dscore = ((e_all[at, :] * scaled) * (dprob - delta) * (1.0 - tanh * tanh)).astype(bf16)
        dkey = nn(dscore, q_two[...]).astype(bf16).reshape(2, BLOCK, HD)
        dvalue = nn(w_all[at, :], grad_two).astype(bf16).reshape(2, BLOCK, HD)
        ga_ref[pl.ds(2 * i, 2)] = jnp.where(odd == 0, dkey, dvalue)
        gb_ref[pl.ds(2 * i, 2)] = jnp.where(odd == 0, dvalue, dkey)
        return carry

    lax.fori_loop(0, tiles, back, 0, unroll=unroll)


def sum_body(which, slots, start, last, meta, lists, counts, *refs):
    given = refs[start : start + len(which)]
    out_ref = refs[start + len(which)]
    total = refs[-1] if last else out_ref
    me = meta[0]
    total[...] = refs[0][...] if start else jnp.zeros_like(total)
    for ref, k in zip(given, which):
        row = me ^ offset(k, meta[2])

        def one(s, carry, ref=ref, row=row):
            at = lists[row, s]
            total[at] += ref[s].astype(f32)
            return carry

        lax.fori_loop(0, counts[row], one, 0)
    if last:
        out_ref[...] = total[...].astype(bf16)


def decay_body(one_ref, two_ref, one_out, two_out):
    one_out[...] = beta_one * one_ref[...]
    two_out[...] = beta_two * two_ref[...]


def adam_body(parts, copies, cut, turns, grad_ref, bank_ref, one_ref, two_ref, *refs):
    outs, made, left = refs[0:3], refs[3], refs[4]
    rows = grad_ref.shape[1] // cut
    lines = rows * parts
    turn = lax.axis_index("mp") if turns else 0

    def take(i, c):
        at = pl.ds(c * lines, lines)
        return pltpu.make_async_copy(made.at[i, at], outs[i].at[at], left.at[i, c])

    for c in range(cut):
        for part in range(parts):
            at = pl.ds(c * rows, rows)
            source = offset(part, turn)
            grad = grad_ref[source, at].astype(f32)
            if copies <= 4:
                for copy in range(1, copies):
                    grad = grad + grad_ref[copy * parts + source, at].astype(f32)
            else:

                def add(copy, run, source=source, at=at):
                    return run + grad_ref[copy * parts + source, at].astype(f32)

                grad = lax.fori_loop(1, copies, add, grad)
            line = part % (parts // 2) * 2 + part // (parts // 2)
            at = pl.ds(c * lines + line, rows, stride=parts)
            moment = one_ref[at, :] + (1.0 - beta_one) * grad
            second = two_ref[at, :] + (1.0 - beta_two) * grad * grad
            made[1, at, :] = moment
            made[2, at, :] = second
            made[0, at, :] = bank_ref[at, :] - learn_rate * (moment / bias_one) / (
                jnp.sqrt(second / bias_two) + adam_eps
            )
        for i in range(3):
            take(i, c).start()
    for c in range(cut):
        for i in range(3):
            take(i, c).wait()


def local(
    queries,
    keys,
    values,
    out_weight,
    out_grad,
    bank,
    moment_one,
    moment_two,
    block_list,
    block_count,
    token_count,
):
    owners = lax.axis_size("req")
    mp_size = lax.axis_size("mp")
    me = lax.axis_index("req")
    tokens = queries.shape[0]
    kv_local = keys.shape[1] // HD
    features = queries.shape[1]
    parts = 2 * kv_local
    copies = owners // parts
    rows = bank.shape[0]
    blocks = rows // BLOCK
    slots = block_list.shape[1]
    wide = 2 * tokens
    smem = pl.BlockSpec(memory_space=pltpu.SMEM)
    vmem = pl.BlockSpec(memory_space=pltpu.VMEM)

    def lines(array):
        four = array.reshape(rows, 2, kv_local, HD).transpose(0, 2, 1, 3)
        return four.reshape(rows * parts, HD)

    def unlines(array):
        four = array.reshape(rows, kv_local, 2, HD).transpose(0, 2, 1, 3)
        return four.reshape(rows, 2, kv_local * HD)

    held_mib = owners * blocks * BLOCK * HD * 2 // MIB
    turns = parts == 8 and mp_size == 2
    place = me & (parts - 1)
    turn = lax.axis_index("mp") if turns else jnp.zeros_like(me)
    label = jnp.where(turn == 1, place // 2 + place % 2 * 4, place)
    meta = jnp.stack([me, token_count[0], turn, label])

    cut = 4
    outgoing = call(
        functools.partial(split_body, parts, copies, turns),
        jax.ShapeDtypeStruct((owners, rows, HD), bf16),
        limit=held_mib + 4,
        in_specs=[vmem],
        out_specs=vmem,
        name="split",
    )(lines(bank))
    spread = lax.all_to_all(outgoing, "req", split_axis=0, concat_axis=0, tiled=True)

    partial = lax.dot_general(
        out_weight, out_grad, (((1,), (1,)), ((), ())), preferred_element_type=f32
    )
    if mp_size == 2:
        side = lax.axis_index("mp")
        theirs = lax.dynamic_slice_in_dim(partial, (1 - side) * features, features, 0)
        mine = lax.dynamic_slice_in_dim(partial, side * features, features, 0)
        head_grad = mine + lax.ppermute(theirs, "mp", [(0, 1), (1, 0)])
    else:
        head_grad = lax.psum_scatter(partial, "mp", scatter_dimension=0, tiled=True)

    piece = jax.ShapeDtypeStruct((slots, BLOCK, HD), bf16)
    def pick(which, after):
        return call(
            functools.partial(pick_body, which, slots),
            [piece] * len(which),
            limit=held_mib + len(which) * slots * BLOCK * HD * 2 // MIB + 2,
            in_specs=[smem, smem, pl.BlockSpec(memory_space=pl.ANY), vmem],
            out_specs=[vmem] * len(which),
            name="pick",
        )(meta, block_list, after, spread.reshape(owners * blocks, BLOCK, HD))

    def swap(array, k):
        if k == 0:
            return array
        pairs = []
        for i in range(owners):
            for core in range(mp_size):
                partner = i ^ (turned(k) if turns and core else k)
                pairs.append((i * mp_size + core, partner * mp_size + core))
        return lax.ppermute(array, ("req", "mp"), pairs)

    fetched = [None] * parts

    def fetch(which, after):
        which = [k for k in which if k < parts]
        if which:
            for k, array in zip(which, pick(which, after)):
                fetched[k] = swap(array, k)

    order = (0, 3, 1, 2) if kv_local == 4 else tuple(range(kv_local))
    phases = [order[: (kv_local + 1) // 2], order[(kv_local + 1) // 2 :]]
    phases = [[k + far for k in phase for far in (0, kv_local)] for phase in phases if phase]
    fetch(phases[0], head_grad)
    for phase in phases[1:]:
        fetch(phase[:2], fetched[kv_local])

    heads_out = None
    returned = [None] * parts
    back = [None] * parts
    for step, near in enumerate(order):
        far = near + kv_local

        def column(i, meta, counts, near=near):
            return (0, (meta[3] ^ near) & (kv_local - 1))

        def line(i, meta, counts, near=near):
            return ((meta[3] ^ near) & (kv_local - 1), 0)

        def whole(i, meta, counts):
            return (0, 0, 0)

        block_spec = pl.BlockSpec((slots, BLOCK, HD), whole)
        in_specs = [
            pl.BlockSpec((tokens, 2 * HD), column),
            pl.BlockSpec((tokens, HD), column),
            pl.BlockSpec((tokens, HD), column),
            pl.BlockSpec((2 * HD, tokens), line),
            block_spec,
            block_spec,
        ]
        operands = [queries, keys, values, head_grad, fetched[near], fetched[far]]
        ahead = [] if step == 0 else [heads_out]
        aliases = {2: 0} if step else {}
        in_specs = [pl.BlockSpec(memory_space=pl.ANY)] * len(ahead) + in_specs
        operands = ahead + operands
        span = slots * BLOCK
        heads_out, returned[near], returned[far] = call(
            functools.partial(head_body, len(ahead), parts, slots),
            [jax.ShapeDtypeStruct((tokens, features), bf16), piece, piece],
            grid_spec=pltpu.PrefetchScalarGridSpec(
                num_scalar_prefetch=2,
                grid=(1,),
                in_specs=in_specs,
                out_specs=[pl.BlockSpec((tokens, 2 * HD), column), block_spec, block_spec],
                scratch_shapes=[
                    pltpu.VMEM((wide, HD), bf16),
                    pltpu.VMEM((span, wide), f32),
                    pltpu.VMEM((span, wide), f32),
                    pltpu.VMEM((span, wide), bf16),
                ],
            ),
            limit=(span * (10 * wide + 16 * HD) + 32 * tokens * HD) // MIB + 8,
            cost=pl.CostEstimate(
                flops=10 * span * wide * HD,
                bytes_accessed=8 * span * HD,
                transcendentals=2 * span * wide,
            ),
            input_output_aliases=aliases,
            name="head",
        )(meta, block_count, *operands)
        for k in (near, far):
            back[k] = swap(returned[k], k)
        if step == 0:
            for phase in phases[1:]:
                fetch(phase[2:], heads_out)

    sums = None
    for phase in phases:
        last = phase is phases[-1]
        start = [] if sums is None else [sums]
        sums = call(
            functools.partial(sum_body, phase, slots, len(start), last),
            jax.ShapeDtypeStruct((owners * blocks, BLOCK, HD), bf16 if last else f32),
            limit=5 * held_mib + len(phase) * slots * BLOCK * HD * 2 // MIB + 2,
            in_specs=[smem] * 3 + [vmem] * (len(start) + len(phase)),
            out_specs=vmem,
            scratch_shapes=[pltpu.VMEM((owners * blocks, BLOCK, HD), f32)] if last else [],
            name="sums",
        )(meta, block_list, block_count, *start, *[back[k] for k in phase])
    grads = lax.all_to_all(
        sums.reshape(owners, rows, HD), "req", split_axis=0, concat_axis=0, tiled=True
    )

    if mp_size == 2:
        other = lax.ppermute(heads_out, "mp", [(0, 1), (1, 0)])
        both = jnp.concatenate(
            [jnp.where(side == 0, heads_out, other), jnp.where(side == 0, other, heads_out)], axis=1
        )
    else:
        both = lax.all_gather(heads_out, "mp", axis=1, tiled=True)
    attn_out = jnp.dot(both, out_weight, preferred_element_type=f32)

    state_out = jax.ShapeDtypeStruct((rows * parts, HD), f32)
    hbm = pl.BlockSpec(memory_space=pl.ANY)
    decayed = call(
        decay_body,
        [pltpu.VMEM(state_out.shape, f32)] * 2,
        limit=6,
        in_specs=[vmem] * 2,
        out_specs=[vmem] * 2,
        name="decay",
    )(lines(moment_one), lines(moment_two))
    bank_next, moment_next, second_next = call(
        functools.partial(adam_body, parts, copies, cut, turns),
        [state_out] * 3,
        limit=10,
        in_specs=[vmem] * 4,
        out_specs=[hbm] * 3,
        scratch_shapes=[
            pltpu.VMEM((3, rows * parts, HD), f32),
            pltpu.SemaphoreType.DMA((3, cut)),
        ],
        name="adam",
    )(grads, lines(bank), *decayed)
    return (attn_out, unlines(bank_next), unlines(moment_next), unlines(second_next))


def solution(mesh):
    return jax.shard_map(
        local,
        mesh=mesh,
        in_specs=(
            P("req", "mp"),
            P("req", "mp"),
            P("req", "mp"),
            P(None, "mp"),
            P("req", "mp"),
            P("req", None, "mp"),
            P("req", None, "mp"),
            P("req", None, "mp"),
            P(),
            P(),
            P("req"),
        ),
        out_specs=(
            P("req", "mp"),
            P("req", None, "mp"),
            P("req", None, "mp"),
            P("req", None, "mp"),
        ),
        check_vma=False,
    )
```

```python
import functools
import math

import jax
import jax.numpy as jnp
from jax import lax
from jax.experimental import pallas as pl
from jax.experimental.pallas import tpu as pltpu
from jax.sharding import PartitionSpec as P

HD = 128
BLOCK = 128

softcap = 50.0
qscale = 1.0 / 12.0
beta_one = 0.9
beta_two = 0.999
learn_rate = 0.3
adam_eps = 1e-08
bias_one = 1.0 - 0.9**10
bias_two = 1.0 - 0.999**10

exponent = softcap * math.log2(math.e)

f32 = jnp.float32
bf16 = jnp.bfloat16
MIB = 1 << 20


def nn(a, b):
    return lax.dot_general(a, b, (((1,), (0,)), ((), ())), preferred_element_type=f32)


def call(body, out, limit, cost=None, **more):
    return pl.pallas_call(
        body,
        out_shape=out,
        compiler_params=pltpu.CompilerParams(vmem_limit_bytes=limit * MIB),
        cost_estimate=cost,
        **more,
    )


def turned(label):
    return (label << 1) % 8 + label // 4


def offset(label, turn):
    return jnp.where(turn == 1, turned(label), label)


def split_body(parts, copies, turns, bank_ref, out_ref):
    rows = out_ref.shape[1]
    turn = lax.axis_index("mp") if turns else 0
    for part in range(parts):
        line = part % (parts // 2) * 2 + part // (parts // 2)
        chunk = bank_ref[pl.ds(line, rows, stride=parts), :].astype(bf16)
        for copy in range(copies):
            out_ref[copy * parts + offset(part, turn)] = chunk


def pick_body(which, slots, meta, lists, _, all_ref, *outs):
    me = meta[0]
    for out, k in zip(outs, which):
        row = me ^ offset(k, meta[2])

        def one(s, carry, out=out, row=row):
            out[s] = all_ref[lists[row, s]]
            return carry

        lax.fori_loop(0, slots, one, 0, unroll=4)


def head_body(near, slots, meta, counts, _, q_all, k_all, v_all, g_all, a_ref, b_ref, *refs):
    ho_ref, ga_ref, gb_ref, q_two, t_all, e_all, w_all = refs
    kv_local = k_all.shape[1] // HD
    head = (meta[3] ^ near) & (kv_local - 1)
    one = pl.ds(pl.multiple_of(head * HD, HD), HD)
    two = pl.ds(pl.multiple_of(head * 2 * HD, 2 * HD), 2 * HD)
    q_ref = q_all.at[:, two]
    k_ref = k_all.at[:, one]
    v_ref = v_all.at[:, one]
    g_ref = g_all.at[two, :]
    tokens = q_ref.shape[0]
    wide = 2 * tokens
    used = counts[meta[0]]
    live_tokens = meta[1]
    odd = meta[3] // kv_local
    tile = 2 * BLOCK
    tiles = slots // 2

    lane = lax.broadcasted_iota(jnp.int32, (1, wide), 1)
    token = jnp.where(lane >= tokens, lane - tokens, lane)
    row_ok = token < live_tokens

    query = q_ref[...]
    q_two[0:tokens, :] = query[:, 0:HD]
    q_two[tokens:wide, :] = query[:, HD : 2 * HD]
    q_t = q_two[...].T
    grad = jnp.concatenate([g_ref[0:HD, :], g_ref[HD : 2 * HD, :]], axis=1)
    grad = jnp.where(row_ok, grad, 0.0).astype(bf16)
    grad_two = grad.T

    def pair(ref_even, ref_odd, i):
        even = ref_even[pl.ds(2 * i, 2)].reshape(tile, HD)
        other = ref_odd[pl.ds(2 * i, 2)].reshape(tile, HD)
        return jnp.where(odd == 0, even, other)

    raw = nn(k_ref[...], q_t)
    row = lax.broadcasted_iota(jnp.int32, (tokens, wide), 0)
    token_exp = jnp.where(row <= token, jnp.exp2(exponent * jnp.tanh(raw * (qscale / softcap))), 0.0)
    total = jnp.sum(token_exp, axis=0, keepdims=True)

    def scores(i, total):
        raw = nn(pair(a_ref, b_ref, i), q_t)
        tanh = jnp.tanh(raw * (qscale / softcap))
        slot = 2 * i + lax.broadcasted_iota(jnp.int32, (tile, 1), 0) // BLOCK
        exps = jnp.where(slot < used, jnp.exp2(exponent * tanh), 0.0)
        at = pl.ds(i * tile, tile)
        t_all[at, :] = tanh
        e_all[at, :] = exps
        return total + jnp.sum(exps, axis=0, keepdims=True)

    unroll = tiles if tiles <= 4 else 1
    total = lax.fori_loop(0, tiles, scores, total, unroll=unroll)
    inverse = 1.0 / total

    mixed = nn(v_ref[...].T, (token_exp * inverse).astype(bf16))

    def mix(i, mixed):
        at = pl.ds(i * tile, tile)
        weights = (e_all[at, :] * inverse).astype(bf16)
        w_all[at, :] = weights
        return mixed + nn(pair(b_ref, a_ref, i).T, weights)

    mixed = lax.fori_loop(0, tiles, mix, mixed, unroll=unroll)
    out = jnp.where(row_ok, mixed, 0.0).astype(bf16)
    delta = jnp.sum(grad.astype(f32) * out.astype(f32), axis=0, keepdims=True)
    ho_ref[:, 0:HD] = out[:, 0:tokens].T
    ho_ref[:, HD : 2 * HD] = out[:, tokens:wide].T
    scaled = inverse * qscale

    def back(i, carry):
        at = pl.ds(i * tile, tile)
        dprob = nn(pair(b_ref, a_ref, i), grad)
        tanh = t_all[at, :]
        dscore = ((e_all[at, :] * scaled) * (dprob - delta) * (1.0 - tanh * tanh)).astype(bf16)
        dkey = nn(dscore, q_two[...]).astype(bf16).reshape(2, BLOCK, HD)
        dvalue = nn(w_all[at, :], grad_two).astype(bf16).reshape(2, BLOCK, HD)
        ga_ref[pl.ds(2 * i, 2)] = jnp.where(odd == 0, dkey, dvalue)
        gb_ref[pl.ds(2 * i, 2)] = jnp.where(odd == 0, dvalue, dkey)
        return carry

    lax.fori_loop(0, tiles, back, 0, unroll=unroll)


def sum_body(which, slots, start, last, meta, lists, counts, *refs):
    given = refs[start : start + len(which)]
    out_ref = refs[start + len(which)]
    total = refs[-1] if last else out_ref
    me = meta[0]
    total[...] = refs[0][...] if start else jnp.zeros_like(total)
    for ref, k in zip(given, which):
        row = me ^ offset(k, meta[2])

        def one(s, carry, ref=ref, row=row):
            at = lists[row, s]
            total[at] += ref[s].astype(f32)
            return carry

        lax.fori_loop(0, counts[row], one, 0)
    if last:
        out_ref[...] = total[...].astype(bf16)


def join_body(order, meta, *refs):
    out_ref = refs[-1]
    width = refs[0].shape[1]
    for near, ref in zip(order, refs):
        head = (meta[3] ^ near) & (len(order) - 1)
        out_ref[:, pl.ds(pl.multiple_of(head * width, width), width)] = ref[...]


def project_body(meta, *refs):
    pieces, (weight_ref, out_ref, x_ref) = refs[:-3], refs[-3:]

    @pl.when(pl.program_id(0) == 0)
    def _():
        width = pieces[0].shape[1]
        for i, ref in enumerate(pieces):
            at = pl.multiple_of((meta[4] ^ i) * width, width) if len(pieces) > 1 else 0
            x_ref[:, pl.ds(at, width)] = ref[...]

    out_ref[...] = nn(x_ref[...], weight_ref[...])


def adam_body(parts, copies, cut, turns, grad_ref, *refs):
    state, outs = refs[0:3], refs[3:6]
    held, made, arrived, left = refs[6:10]
    rows = grad_ref.shape[1] // cut
    lines = rows * parts
    turn = lax.axis_index("mp") if turns else 0

    def bring(i, c):
        at = pl.ds(c * lines, lines)
        return pltpu.make_async_copy(state[i].at[at], held.at[i, at], arrived.at[i, c])

    def take(i, c):
        at = pl.ds(c * lines, lines)
        return pltpu.make_async_copy(made.at[i, at], outs[i].at[at], left.at[i, c])

    for c in range(cut):
        for i in range(3):
            bring(i, c).start()
    for c in range(cut):
        for i in range(3):
            bring(i, c).wait()
        for part in range(parts):
            at = pl.ds(c * rows, rows)
            source = offset(part, turn)
            grad = grad_ref[source, at].astype(f32)
            if copies <= 4:
                for copy in range(1, copies):
                    grad = grad + grad_ref[copy * parts + source, at].astype(f32)
            else:

                def add(copy, run, source=source, at=at):
                    return run + grad_ref[copy * parts + source, at].astype(f32)

                grad = lax.fori_loop(1, copies, add, grad)
            line = part % (parts // 2) * 2 + part // (parts // 2)
            at = pl.ds(c * lines + line, rows, stride=parts)
            moment = beta_one * held[1, at, :] + (1.0 - beta_one) * grad
            second = beta_two * held[2, at, :] + (1.0 - beta_two) * grad * grad
            made[1, at, :] = moment
            made[2, at, :] = second
            made[0, at, :] = held[0, at, :] - learn_rate * (moment / bias_one) / (
                jnp.sqrt(second / bias_two) + adam_eps
            )
        for i in range(3):
            take(i, c).start()
    for c in range(cut):
        for i in range(3):
            take(i, c).wait()


def local(
    queries,
    keys,
    values,
    out_weight,
    out_grad,
    bank,
    moment_one,
    moment_two,
    block_list,
    block_count,
    token_count,
):
    owners = lax.axis_size("req")
    mp_size = lax.axis_size("mp")
    me = lax.axis_index("req")
    tokens = queries.shape[0]
    kv_local = keys.shape[1] // HD
    features = queries.shape[1]
    parts = 2 * kv_local
    copies = owners // parts
    rows = bank.shape[0]
    blocks = rows // BLOCK
    slots = block_list.shape[1]
    wide = 2 * tokens
    smem = pl.BlockSpec(memory_space=pltpu.SMEM)
    vmem = pl.BlockSpec(memory_space=pltpu.VMEM)
    hbm = pl.BlockSpec(memory_space=pl.ANY)

    def lines(array):
        four = array.reshape(rows, 2, kv_local, HD).transpose(0, 2, 1, 3)
        return four.reshape(rows * parts, HD)

    def unlines(array):
        four = array.reshape(rows, kv_local, 2, HD).transpose(0, 2, 1, 3)
        return four.reshape(rows, 2, kv_local * HD)

    held_mib = owners * blocks * BLOCK * HD * 2 // MIB
    turns = parts == 8 and mp_size == 2
    place = me & (parts - 1)
    turn = lax.axis_index("mp") if turns else jnp.zeros_like(me)
    label = jnp.where(turn == 1, place // 2 + place % 2 * 4, place)
    meta = jnp.stack([me, token_count[0], turn, label, lax.axis_index("mp")])

    cut = 4
    outgoing = call(
        functools.partial(split_body, parts, copies, turns),
        jax.ShapeDtypeStruct((owners, rows, HD), bf16),
        limit=held_mib + 4,
        in_specs=[vmem],
        out_specs=vmem,
        name="split",
    )(lines(bank))
    spread = lax.all_to_all(outgoing, "req", split_axis=0, concat_axis=0, tiled=True)

    partial = lax.dot_general(
        out_weight, out_grad, (((1,), (1,)), ((), ())), preferred_element_type=f32
    )
    if mp_size == 2:
        side = lax.axis_index("mp")
        theirs = lax.dynamic_slice_in_dim(partial, (1 - side) * features, features, 0)
        mine = lax.dynamic_slice_in_dim(partial, side * features, features, 0)
        head_grad = mine + lax.ppermute(theirs, "mp", [(0, 1), (1, 0)])
    else:
        head_grad = lax.psum_scatter(partial, "mp", scatter_dimension=0, tiled=True)

    piece = jax.ShapeDtypeStruct((slots, BLOCK, HD), bf16)
    def pick(which, after):
        return call(
            functools.partial(pick_body, which, slots),
            [piece] * len(which),
            limit=held_mib + len(which) * slots * BLOCK * HD * 2 // MIB + 2,
            in_specs=[smem, smem, pl.BlockSpec(memory_space=pl.ANY), vmem],
            out_specs=[vmem] * len(which),
            name="pick",
        )(meta, block_list, after, spread.reshape(owners * blocks, BLOCK, HD))

    def swap(array, k):
        if k == 0:
            return array
        pairs = []
        for i in range(owners):
            for core in range(mp_size):
                partner = i ^ (turned(k) if turns and core else k)
                pairs.append((i * mp_size + core, partner * mp_size + core))
        return lax.ppermute(array, ("req", "mp"), pairs)

    fetched = [None] * parts

    def fetch(which, after):
        which = [k for k in which if k < parts]
        if which:
            for k, array in zip(which, pick(which, after)):
                fetched[k] = swap(array, k)

    order = (0, 2, 1, 3) if kv_local == 4 else tuple(range(kv_local))
    phases = [order[: (kv_local + 1) // 2], order[(kv_local + 1) // 2 :]]
    phases = [[k + far for k in phase for far in (0, kv_local)] for phase in phases if phase]
    fetch(phases[0], head_grad)
    for phase in phases[1:]:
        fetch(phase[:2], fetched[kv_local])

    span = slots * BLOCK
    heads = []
    returned = [None] * parts
    back = [None] * parts
    for step, near in enumerate(order):
        far = near + kv_local
        out, returned[near], returned[far] = call(
            functools.partial(head_body, near, slots),
            [jax.ShapeDtypeStruct((tokens, 2 * HD), bf16), piece, piece],
            limit=(span * (10 * wide + 8 * HD) + 8 * tokens * features) // MIB + 8,
            in_specs=[smem, smem, hbm] + [vmem] * 6,
            out_specs=[vmem] * 3,
            scratch_shapes=[
                pltpu.VMEM((wide, HD), bf16),
                pltpu.VMEM((span, wide), f32),
                pltpu.VMEM((span, wide), f32),
                pltpu.VMEM((span, wide), bf16),
            ],
            cost=pl.CostEstimate(
                flops=10 * span * wide * HD,
                bytes_accessed=8 * span * HD,
                transcendentals=2 * span * wide,
            ),
            name="head",
        )(
            meta,
            block_count,
            heads[-1] if heads else block_count,
            queries,
            keys,
            values,
            head_grad,
            fetched[near],
            fetched[far],
        )
        heads.append(out)
        for k in (near, far):
            back[k] = swap(returned[k], k)
        if step == 0:
            for phase in phases[1:]:
                fetch(phase[2:], out)

    sums = None
    for phase in phases:
        last = phase is phases[-1]
        start = [] if sums is None else [sums]
        sums = call(
            functools.partial(sum_body, phase, slots, len(start), last),
            jax.ShapeDtypeStruct((owners * blocks, BLOCK, HD), bf16 if last else f32),
            limit=5 * held_mib + len(phase) * slots * BLOCK * HD * 2 // MIB + 2,
            in_specs=[smem] * 3 + [vmem] * (len(start) + len(phase)),
            out_specs=vmem,
            scratch_shapes=[pltpu.VMEM((owners * blocks, BLOCK, HD), f32)] if last else [],
            name="sums",
        )(meta, block_list, block_count, *start, *[back[k] for k in phase])
    grads = lax.all_to_all(
        sums.reshape(owners, rows, HD), "req", split_axis=0, concat_axis=0, tiled=True
    )

    heads_out = heads[0]
    if kv_local > 1:
        heads_out = call(
            functools.partial(join_body, order),
            jax.ShapeDtypeStruct((tokens, features), bf16),
            limit=4,
            in_specs=[smem] + [vmem] * kv_local,
            out_specs=vmem,
            name="join",
        )(meta, *heads)
    if mp_size == 2:
        both = [heads_out, lax.ppermute(heads_out, "mp", [(0, 1), (1, 0)])]
    else:
        both = [lax.all_gather(heads_out, "mp", axis=1, tiled=True)]
    inner, columns = out_weight.shape
    strip = 384 if columns % 384 == 0 else columns
    attn_out = call(
        project_body,
        jax.ShapeDtypeStruct((tokens, columns), f32),
        limit=14,
        grid=(columns // strip,),
        in_specs=[smem]
        + [pl.BlockSpec(x.shape, lambda i: (0, 0)) for x in both]
        + [pl.BlockSpec((inner, strip), lambda i: (0, i))],
        out_specs=pl.BlockSpec((tokens, strip), lambda i: (0, i)),
        scratch_shapes=[pltpu.VMEM((tokens, inner), bf16)],
        cost=pl.CostEstimate(
            flops=2 * tokens * inner * columns,
            bytes_accessed=2 * inner * columns + 4 * tokens * columns,
            transcendentals=0,
        ),
        name="project",
    )(meta, *both, out_weight)

    state_out = jax.ShapeDtypeStruct((rows * parts, HD), f32)
    bank_next, moment_next, second_next = call(
        functools.partial(adam_body, parts, copies, cut, turns),
        [state_out] * 3,
        limit=10,
        in_specs=[vmem] + [hbm] * 3,
        out_specs=[hbm] * 3,
        scratch_shapes=[
            pltpu.VMEM((3, rows * parts, HD), f32),
            pltpu.VMEM((3, rows * parts, HD), f32),
            pltpu.SemaphoreType.DMA((3, cut)),
            pltpu.SemaphoreType.DMA((3, cut)),
        ],
        name="adam",
    )(grads, *[pltpu.with_memory_space_constraint(lines(x), pltpu.HBM) for x in (bank, moment_one, moment_two)])
    return (attn_out, unlines(bank_next), unlines(moment_next), unlines(second_next))


def solution(mesh):
    return jax.shard_map(
        local,
        mesh=mesh,
        in_specs=(
            P("req", "mp"),
            P("req", "mp"),
            P("req", "mp"),
            P(None, "mp"),
            P("req", "mp"),
            P("req", None, "mp"),
            P("req", None, "mp"),
            P("req", None, "mp"),
            P(),
            P(),
            P("req"),
        ),
        out_specs=(
            P("req", "mp"),
            P("req", None, "mp"),
            P("req", None, "mp"),
            P("req", None, "mp"),
        ),
        check_vma=False,
    )
```

```python
import functools
import math

import jax
import jax.numpy as jnp
from jax import lax
from jax.experimental import pallas as pl
from jax.experimental.pallas import tpu as pltpu
from jax.sharding import PartitionSpec as P

HD = 128
BLOCK = 128

softcap = 50.0
qscale = 1.0 / 12.0
beta_one = 0.9
beta_two = 0.999
learn_rate = 0.3
adam_eps = 1e-08
bias_one = 1.0 - 0.9**10
bias_two = 1.0 - 0.999**10

exponent = softcap * math.log2(math.e)

f32 = jnp.float32
bf16 = jnp.bfloat16
MIB = 1 << 20


def nn(a, b):
    return lax.dot_general(a, b, (((1,), (0,)), ((), ())), preferred_element_type=f32)


def call(body, out, limit, cost=None, **more):
    return pl.pallas_call(
        body,
        out_shape=out,
        compiler_params=pltpu.CompilerParams(vmem_limit_bytes=limit * MIB),
        cost_estimate=cost,
        **more,
    )


BITS = ((1, 0, 2), (2, 1, 0))


def place_of(label, core):
    return sum((label >> j & 1) << bit for j, bit in enumerate(BITS[core]))


def label_of(place, core):
    return sum((place >> bit & 1) << j for j, bit in enumerate(BITS[core]))


def offset(label, turn):
    placed = jnp.where(turn == 1, place_of(label, 1), place_of(label, 0))
    return jnp.where(turn == 2, label, placed)


def split_body(parts, copies, cut, turns, bank_ref, out_ref, held, made, arrived, left):
    rows = out_ref.shape[1] // cut
    lines = rows * parts
    turn = lax.axis_index("mp") if turns else 2

    def bring(c):
        at = pl.ds(c * lines, lines)
        return pltpu.make_async_copy(bank_ref.at[at], held.at[at], arrived.at[c])

    def give(c, copy):
        at = pl.ds(c * rows, rows)
        to = out_ref.at[pl.ds(copy * parts, parts), at]
        return pltpu.make_async_copy(made.at[:, at], to, left.at[c, copy])

    for c in range(cut):
        bring(c).start()
    for c in range(cut):
        bring(c).wait()
        for part in range(parts):
            line = part % (parts // 2) * 2 + part // (parts // 2)
            chunk = held[pl.ds(c * lines + line, rows, stride=parts), :].astype(bf16)
            made[offset(part, turn), pl.ds(c * rows, rows)] = chunk
        for copy in range(copies):
            give(c, copy).start()
    for c in range(cut):
        for copy in range(copies):
            give(c, copy).wait()


def pick_body(which, slots, meta, lists, _, all_ref, *outs):
    me = meta[0]
    for out, k in zip(outs, which):
        row = me ^ offset(k, meta[2])

        def one(s, carry, out=out, row=row):
            out[s] = all_ref[lists[row, s]]
            return carry

        lax.fori_loop(0, slots, one, 0, unroll=4)


def head_body(near, slots, meta, counts, _, q_all, k_all, v_all, g_all, a_ref, b_ref, *refs):
    ho_ref, ga_ref, gb_ref, q_two, t_all, e_all, w_all = refs
    kv_local = k_all.shape[1] // HD
    head = (meta[3] ^ near) & (kv_local - 1)
    one = pl.ds(pl.multiple_of(head * HD, HD), HD)
    two = pl.ds(pl.multiple_of(head * 2 * HD, 2 * HD), 2 * HD)
    q_ref = q_all.at[:, two]
    k_ref = k_all.at[:, one]
    v_ref = v_all.at[:, one]
    g_ref = g_all.at[two, :]
    tokens = q_ref.shape[0]
    wide = 2 * tokens
    used = counts[meta[0]]
    live_tokens = meta[1]
    odd = meta[3] // kv_local
    tile = 2 * BLOCK
    tiles = slots // 2

    lane = lax.broadcasted_iota(jnp.int32, (1, wide), 1)
    token = jnp.where(lane >= tokens, lane - tokens, lane)
    row_ok = token < live_tokens

    query = q_ref[...]
    q_two[0:tokens, :] = query[:, 0:HD]
    q_two[tokens:wide, :] = query[:, HD : 2 * HD]
    q_t = q_two[...].T
    grad = jnp.concatenate([g_ref[0:HD, :], g_ref[HD : 2 * HD, :]], axis=1)
    grad = jnp.where(row_ok, grad, 0.0).astype(bf16)
    grad_two = grad.T

    def pair(ref_even, ref_odd, i):
        even = ref_even[pl.ds(2 * i, 2)].reshape(tile, HD)
        other = ref_odd[pl.ds(2 * i, 2)].reshape(tile, HD)
        return jnp.where(odd == 0, even, other)

    raw = nn(k_ref[...], q_t)
    row = lax.broadcasted_iota(jnp.int32, (tokens, wide), 0)
    token_exp = jnp.where(row <= token, jnp.exp2(exponent * jnp.tanh(raw * (qscale / softcap))), 0.0)
    total = jnp.sum(token_exp, axis=0, keepdims=True)

    def scores(i, total):
        raw = nn(pair(a_ref, b_ref, i), q_t)
        tanh = jnp.tanh(raw * (qscale / softcap))
        slot = 2 * i + lax.broadcasted_iota(jnp.int32, (tile, 1), 0) // BLOCK
        exps = jnp.where(slot < used, jnp.exp2(exponent * tanh), 0.0)
        at = pl.ds(i * tile, tile)
        t_all[at, :] = tanh
        e_all[at, :] = exps
        return total + jnp.sum(exps, axis=0, keepdims=True)

    unroll = tiles if tiles <= 4 else 1
    total = lax.fori_loop(0, tiles, scores, total, unroll=unroll)
    inverse = 1.0 / total

    mixed = nn(v_ref[...].T, (token_exp * inverse).astype(bf16))

    def mix(i, mixed):
        at = pl.ds(i * tile, tile)
        weights = (e_all[at, :] * inverse).astype(bf16)
        w_all[at, :] = weights
        return mixed + nn(pair(b_ref, a_ref, i).T, weights)

    mixed = lax.fori_loop(0, tiles, mix, mixed, unroll=unroll)
    out = jnp.where(row_ok, mixed, 0.0).astype(bf16)
    delta = jnp.sum(grad.astype(f32) * out.astype(f32), axis=0, keepdims=True)
    ho_ref[:, 0:HD] = out[:, 0:tokens].T
    ho_ref[:, HD : 2 * HD] = out[:, tokens:wide].T
    scaled = inverse * qscale

    def back(i, carry):
        at = pl.ds(i * tile, tile)
        dprob = nn(pair(b_ref, a_ref, i), grad)
        tanh = t_all[at, :]
        dscore = ((e_all[at, :] * scaled) * (dprob - delta) * (1.0 - tanh * tanh)).astype(bf16)
        dkey = nn(dscore, q_two[...]).astype(bf16).reshape(2, BLOCK, HD)
        dvalue = nn(w_all[at, :], grad_two).astype(bf16).reshape(2, BLOCK, HD)
        ga_ref[pl.ds(2 * i, 2)] = jnp.where(odd == 0, dkey, dvalue)
        gb_ref[pl.ds(2 * i, 2)] = jnp.where(odd == 0, dvalue, dkey)
        return carry

    lax.fori_loop(0, tiles, back, 0, unroll=unroll)


def sum_body(which, slots, start, last, meta, lists, counts, *refs):
    given = refs[start : start + len(which)]
    out_ref = refs[start + len(which)]
    total = refs[-1] if last else out_ref
    me = meta[0]
    total[...] = refs[0][...] if start else jnp.zeros_like(total)
    for ref, k in zip(given, which):
        row = me ^ offset(k, meta[2])

        def one(s, carry, ref=ref, row=row):
            at = lists[row, s]
            total[at] += ref[s].astype(f32)
            return carry

        lax.fori_loop(0, counts[row], one, 0)
    if last:
        out_ref[...] = total[...].astype(bf16)


def join_body(order, meta, *refs):
    out_ref = refs[-1]
    width = refs[0].shape[1]
    for near, ref in zip(order, refs):
        head = (meta[3] ^ near) & (len(order) - 1)
        out_ref[:, pl.ds(pl.multiple_of(head * width, width), width)] = ref[...]


def project_body(meta, *refs):
    pieces, (weight_ref, out_ref, x_ref) = refs[:-3], refs[-3:]

    @pl.when(pl.program_id(0) == 0)
    def _():
        width = pieces[0].shape[1]
        for i, ref in enumerate(pieces):
            at = pl.multiple_of((meta[4] ^ i) * width, width) if len(pieces) > 1 else 0
            x_ref[:, pl.ds(at, width)] = ref[...]

    out_ref[...] = nn(x_ref[...], weight_ref[...])


def adam_body(parts, copies, cut, turns, grad_ref, *refs):
    state, outs = refs[0:3], refs[3:6]
    held, made, arrived, left = refs[6:10]
    rows = grad_ref.shape[1] // cut
    lines = rows * parts
    turn = lax.axis_index("mp") if turns else 2

    def bring(i, c):
        at = pl.ds(c * lines, lines)
        return pltpu.make_async_copy(state[i].at[at], held.at[i, at], arrived.at[i, c])

    def take(i, c):
        at = pl.ds(c * lines, lines)
        return pltpu.make_async_copy(made.at[i, at], outs[i].at[at], left.at[i, c])

    for c in range(cut):
        for i in range(3):
            bring(i, c).start()
    for c in range(cut):
        for i in range(3):
            bring(i, c).wait()
        for part in range(parts):
            at = pl.ds(c * rows, rows)
            source = offset(part, turn)
            grad = grad_ref[source, at].astype(f32)
            if copies <= 4:
                for copy in range(1, copies):
                    grad = grad + grad_ref[copy * parts + source, at].astype(f32)
            else:

                def add(copy, run, source=source, at=at):
                    return run + grad_ref[copy * parts + source, at].astype(f32)

                grad = lax.fori_loop(1, copies, add, grad)
            line = part % (parts // 2) * 2 + part // (parts // 2)
            at = pl.ds(c * lines + line, rows, stride=parts)
            moment = beta_one * held[1, at, :] + (1.0 - beta_one) * grad
            second = beta_two * held[2, at, :] + (1.0 - beta_two) * grad * grad
            made[1, at, :] = moment
            made[2, at, :] = second
            made[0, at, :] = held[0, at, :] - (learn_rate / bias_one) * moment / (
                jnp.sqrt(second * (1.0 / bias_two)) + adam_eps
            )
        for i in range(3):
            take(i, c).start()
    for c in range(cut):
        for i in range(3):
            take(i, c).wait()


def local(
    queries,
    keys,
    values,
    out_weight,
    out_grad,
    bank,
    moment_one,
    moment_two,
    block_list,
    block_count,
    token_count,
):
    owners = lax.axis_size("req")
    mp_size = lax.axis_size("mp")
    me = lax.axis_index("req")
    tokens = queries.shape[0]
    kv_local = keys.shape[1] // HD
    features = queries.shape[1]
    parts = 2 * kv_local
    copies = owners // parts
    rows = bank.shape[0]
    blocks = rows // BLOCK
    slots = block_list.shape[1]
    wide = 2 * tokens
    smem = pl.BlockSpec(memory_space=pltpu.SMEM)
    vmem = pl.BlockSpec(memory_space=pltpu.VMEM)
    hbm = pl.BlockSpec(memory_space=pl.ANY)

    def lines(array):
        four = array.reshape(rows, 2, kv_local, HD).transpose(0, 2, 1, 3)
        return four.reshape(rows * parts, HD)

    def unlines(array):
        four = array.reshape(rows, kv_local, 2, HD).transpose(0, 2, 1, 3)
        return four.reshape(rows, 2, kv_local * HD)

    held_mib = owners * blocks * BLOCK * HD * 2 // MIB
    turns = parts == 8 and mp_size == 2
    place = me & (parts - 1)
    turn = lax.axis_index("mp") if turns else jnp.full_like(me, 2)
    label = jnp.where(turn == 1, label_of(place, 1), label_of(place, 0)) if turns else place
    meta = jnp.stack([me, token_count[0], turn, label, lax.axis_index("mp")])

    cut = 4
    outgoing = call(
        functools.partial(split_body, parts, copies, cut, turns),
        jax.ShapeDtypeStruct((owners, rows, HD), bf16),
        limit=6,
        in_specs=[hbm],
        out_specs=hbm,
        scratch_shapes=[
            pltpu.VMEM((rows * parts, HD), f32),
            pltpu.VMEM((parts, rows, HD), bf16),
            pltpu.SemaphoreType.DMA((cut,)),
            pltpu.SemaphoreType.DMA((cut, copies)),
        ],
        name="split",
    )(pltpu.with_memory_space_constraint(lines(bank), pltpu.HBM))
    spread = lax.all_to_all(outgoing, "req", split_axis=0, concat_axis=0, tiled=True)

    partial = lax.dot_general(
        out_weight, out_grad, (((1,), (1,)), ((), ())), preferred_element_type=f32
    )
    if mp_size == 2:
        side = lax.axis_index("mp")
        theirs = lax.dynamic_slice_in_dim(partial, (1 - side) * features, features, 0)
        mine = lax.dynamic_slice_in_dim(partial, side * features, features, 0)
        head_grad = mine + lax.ppermute(theirs, "mp", [(0, 1), (1, 0)])
    else:
        head_grad = lax.psum_scatter(partial, "mp", scatter_dimension=0, tiled=True)

    piece = jax.ShapeDtypeStruct((slots, BLOCK, HD), bf16)
    def pick(which, after):
        return call(
            functools.partial(pick_body, which, slots),
            [piece] * len(which),
            limit=held_mib + len(which) * slots * BLOCK * HD * 2 // MIB + 2,
            in_specs=[smem, smem, pl.BlockSpec(memory_space=pl.ANY), vmem],
            out_specs=[vmem] * len(which),
            name="pick",
        )(meta, block_list, after, spread.reshape(owners * blocks, BLOCK, HD))

    def swap(array, k):
        if k == 0:
            return array
        pairs = []
        for i in range(owners):
            for core in range(mp_size):
                partner = i ^ (place_of(k, core) if turns else k)
                pairs.append((i * mp_size + core, partner * mp_size + core))
        return lax.ppermute(array, ("req", "mp"), pairs)

    fetched = [None] * parts

    def fetch(which, after):
        which = [k for k in which if k < parts]
        if which:
            for k, array in zip(which, pick(which, after)):
                fetched[k] = swap(array, k)

    order = (0, 1, 2, 3) if kv_local == 4 else tuple(range(kv_local))
    phases = [order[: (kv_local + 1) // 2], order[(kv_local + 1) // 2 :]]
    phases = [[k + far for k in phase for far in (0, kv_local)] for phase in phases if phase]
    fetch(phases[0], head_grad)
    for phase in phases[1:]:
        fetch(phase[:2], fetched[kv_local])

    span = slots * BLOCK
    heads = []
    returned = [None] * parts
    back = [None] * parts
    for step, near in enumerate(order):
        far = near + kv_local
        out, returned[near], returned[far] = call(
            functools.partial(head_body, near, slots),
            [jax.ShapeDtypeStruct((tokens, 2 * HD), bf16), piece, piece],
            limit=(span * (10 * wide + 8 * HD) + 8 * tokens * features) // MIB + 8,
            in_specs=[smem, smem, hbm] + [vmem] * 6,
            out_specs=[vmem] * 3,
            scratch_shapes=[
                pltpu.VMEM((wide, HD), bf16),
                pltpu.VMEM((span, wide), f32),
                pltpu.VMEM((span, wide), f32),
                pltpu.VMEM((span, wide), bf16),
            ],
            cost=pl.CostEstimate(
                flops=10 * span * wide * HD,
                bytes_accessed=8 * span * HD,
                transcendentals=2 * span * wide,
            ),
            name="head",
        )(
            meta,
            block_count,
            heads[-1] if heads else block_count,
            queries,
            keys,
            values,
            head_grad,
            fetched[near],
            fetched[far],
        )
        heads.append(out)
        for k in (near, far):
            back[k] = swap(returned[k], k)
        if step == 0:
            for phase in phases[1:]:
                fetch(phase[2:], out)

    sums = None
    for phase in phases:
        last = phase is phases[-1]
        start = [] if sums is None else [sums]
        sums = call(
            functools.partial(sum_body, phase, slots, len(start), last),
            jax.ShapeDtypeStruct((owners * blocks, BLOCK, HD), bf16 if last else f32),
            limit=5 * held_mib + len(phase) * slots * BLOCK * HD * 2 // MIB + 2,
            in_specs=[smem] * 3 + [vmem] * (len(start) + len(phase)),
            out_specs=vmem,
            scratch_shapes=[pltpu.VMEM((owners * blocks, BLOCK, HD), f32)] if last else [],
            name="sums",
        )(meta, block_list, block_count, *start, *[back[k] for k in phase])
    grads = lax.all_to_all(
        sums.reshape(owners, rows, HD), "req", split_axis=0, concat_axis=0, tiled=True
    )

    heads_out = heads[0]
    if kv_local > 1:
        heads_out = call(
            functools.partial(join_body, order),
            jax.ShapeDtypeStruct((tokens, features), bf16),
            limit=4,
            in_specs=[smem] + [vmem] * kv_local,
            out_specs=vmem,
            name="join",
        )(meta, *heads)
    if mp_size == 2:
        both = [heads_out, lax.ppermute(heads_out, "mp", [(0, 1), (1, 0)])]
    else:
        both = [lax.all_gather(heads_out, "mp", axis=1, tiled=True)]
    inner, columns = out_weight.shape
    strip = 384 if columns % 384 == 0 else columns
    attn_out = call(
        project_body,
        jax.ShapeDtypeStruct((tokens, columns), f32),
        limit=14,
        grid=(columns // strip,),
        in_specs=[smem]
        + [pl.BlockSpec(x.shape, lambda i: (0, 0)) for x in both]
        + [pl.BlockSpec((inner, strip), lambda i: (0, i))],
        out_specs=pl.BlockSpec((tokens, strip), lambda i: (0, i)),
        scratch_shapes=[pltpu.VMEM((tokens, inner), bf16)],
        cost=pl.CostEstimate(
            flops=2 * tokens * inner * columns,
            bytes_accessed=2 * inner * columns + 4 * tokens * columns,
            transcendentals=0,
        ),
        name="project",
    )(meta, *both, out_weight)

    state_out = jax.ShapeDtypeStruct((rows * parts, HD), f32)
    bank_next, moment_next, second_next = call(
        functools.partial(adam_body, parts, copies, cut, turns),
        [state_out] * 3,
        limit=10,
        in_specs=[vmem] + [hbm] * 3,
        out_specs=[hbm] * 3,
        scratch_shapes=[
            pltpu.VMEM((3, rows * parts, HD), f32),
            pltpu.VMEM((3, rows * parts, HD), f32),
            pltpu.SemaphoreType.DMA((3, cut)),
            pltpu.SemaphoreType.DMA((3, cut)),
        ],
        name="adam",
    )(grads, *[pltpu.with_memory_space_constraint(lines(x), pltpu.HBM) for x in (bank, moment_one, moment_two)])
    return (attn_out, unlines(bank_next), unlines(moment_next), unlines(second_next))


def solution(mesh):
    return jax.shard_map(
        local,
        mesh=mesh,
        in_specs=(
            P("req", "mp"),
            P("req", "mp"),
            P("req", "mp"),
            P(None, "mp"),
            P("req", "mp"),
            P("req", None, "mp"),
            P("req", None, "mp"),
            P("req", None, "mp"),
            P(),
            P(),
            P("req"),
        ),
        out_specs=(
            P("req", "mp"),
            P("req", None, "mp"),
            P("req", None, "mp"),
            P("req", None, "mp"),
        ),
        check_vma=False,
    )
```

```python
import functools
import math

import jax
import jax.numpy as jnp
from jax import lax
from jax.experimental import pallas as pl
from jax.experimental.pallas import tpu as pltpu
from jax.sharding import PartitionSpec as P

HD = 128
BLOCK = 128

softcap = 50.0
qscale = 1.0 / 12.0
beta_one = 0.9
beta_two = 0.999
learn_rate = 0.3
adam_eps = 1e-08
bias_one = 1.0 - 0.9**10
bias_two = 1.0 - 0.999**10

exponent = softcap * math.log2(math.e)

f32 = jnp.float32
bf16 = jnp.bfloat16
MIB = 1 << 20


def nn(a, b):
    return lax.dot_general(a, b, (((1,), (0,)), ((), ())), preferred_element_type=f32)


def call(body, out, limit, cost=None, **more):
    return pl.pallas_call(
        body,
        out_shape=out,
        compiler_params=pltpu.CompilerParams(vmem_limit_bytes=limit * MIB),
        cost_estimate=cost,
        **more,
    )


BITS = ((1, 0, 2), (2, 1, 0))


def place_of(label, core):
    return sum((label >> j & 1) << bit for j, bit in enumerate(BITS[core]))


def label_of(place, core):
    return sum((place >> bit & 1) << j for j, bit in enumerate(BITS[core]))


def offset(label, turn):
    placed = jnp.where(turn == 1, place_of(label, 1), place_of(label, 0))
    return jnp.where(turn == 2, label, placed)


def split_body(parts, copies, cut, turns, bank_ref, out_ref, held, made, arrived, left):
    rows = out_ref.shape[1] // cut
    lines = rows * parts
    turn = lax.axis_index("mp") if turns else 2

    def bring(c):
        at = pl.ds(c * lines, lines)
        return pltpu.make_async_copy(bank_ref.at[at], held.at[at], arrived.at[c])

    def give(c, copy):
        at = pl.ds(c * rows, rows)
        to = out_ref.at[pl.ds(copy * parts, parts), at]
        return pltpu.make_async_copy(made.at[:, at], to, left.at[c, copy])

    for c in range(cut):
        bring(c).start()
    for c in range(cut):
        bring(c).wait()
        for part in range(parts):
            line = part % (parts // 2) * 2 + part // (parts // 2)
            chunk = held[pl.ds(c * lines + line, rows, stride=parts), :].astype(bf16)
            made[offset(part, turn), pl.ds(c * rows, rows)] = chunk
        for copy in range(copies):
            give(c, copy).start()
    for c in range(cut):
        for copy in range(copies):
            give(c, copy).wait()


def pick_body(which, slots, meta, lists, _, all_ref, *outs):
    me = meta[0]
    for out, k in zip(outs, which):
        row = me ^ offset(k, meta[2])

        def one(s, carry, out=out, row=row):
            out[s] = all_ref[lists[row, s]]
            return carry

        lax.fori_loop(0, slots, one, 0, unroll=4)


def head_body(near, slots, meta, counts, _, q_all, k_all, v_all, g_all, a_ref, b_ref, *refs):
    ho_ref, ga_ref, gb_ref, q_two, v_two, e_all, c_all = refs
    tokens = q_all.shape[0]
    kv_local = k_all.shape[1] // HD
    head = (meta[3] ^ near) & (kv_local - 1)
    one = pl.ds(pl.multiple_of(head * HD, HD), HD)
    two = pl.ds(pl.multiple_of(head * 2 * HD, 2 * HD), 2 * HD)
    wide = 2 * tokens
    used = counts[meta[0]]
    odd = meta[3] // kv_local
    tile = 128
    lanes = 512
    tiles = slots * BLOCK // tile
    deep = 256
    per = BLOCK // tile
    always = slots * 3 // 5

    query = q_all[:, two]
    q_two[0:tokens, :] = query[:, 0:HD]
    q_two[tokens:wide, :] = query[:, HD : 2 * HD]
    q_t = q_two[...].T
    lane = lax.broadcasted_iota(jnp.int32, (1, wide), 1)
    token = jnp.where(lane >= tokens, lane - tokens, lane)
    row_ok = token < meta[1]
    both = g_all[two, :]
    grad = jnp.concatenate([both[0:HD, :], both[HD : 2 * HD, :]], axis=1)
    grad = jnp.where(row_ok, grad, 0.0).astype(bf16)

    ones = lax.broadcasted_iota(jnp.int32, (tile, HD), 1) < 3
    ones = jnp.where(ones, 1.0, 0.0).astype(bf16)

    def piece(ref_even, ref_odd, i):
        if per == 1:
            return jnp.where(odd == 0, ref_even[i], ref_odd[i])
        at = pl.ds(i % per * tile, tile)
        return jnp.where(odd == 0, ref_even[i // per, at], ref_odd[i // per, at])

    def weigh(key, cols):
        tanh = jnp.tanh(nn(key, q_t[:, cols]) * (qscale / softcap))
        return tanh, jnp.exp2(exponent * tanh)

    span = slots * BLOCK

    def start(cols):
        total = jnp.zeros((1, lanes), f32)
        for i in range(tokens // tile):
            at = pl.ds(i * tile, tile)
            _, exps = weigh(k_all[at, one], cols)
            row = i * tile + lax.broadcasted_iota(jnp.int32, (tile, lanes), 0)
            exps = jnp.where(row <= token[:, cols], exps, 0.0)
            total = total + jnp.sum(exps, axis=0, keepdims=True)
            e_all[pl.ds(span + i * tile, tile), cols] = exps.astype(bf16)
            if cols.start == 0:
                v_two[pl.ds(span + i * tile, tile), 0:HD] = v_all[at, one]
        return total

    def scores(i, total, cols, masked):
        at = pl.ds(i * tile, tile)
        tanh, exps = weigh(piece(a_ref, b_ref, i), cols)
        if masked:
            exps = exps * jnp.where(i // per < used, 1.0, 0.0)
        if cols.start == 0:
            v_two[at, 0:HD] = piece(b_ref, a_ref, i)
            v_two[at, HD : 2 * HD] = ones
        e_all[at, cols] = exps.astype(bf16)
        c_all[at, cols] = exps * (1.0 - tanh * tanh)
        return total + jnp.sum(exps, axis=0, keepdims=True)

    unrolled = slots <= 8
    bands = [slice(at, at + lanes) for at in range(0, wide, lanes)]
    inverse, outs = [], []
    for cols in bands:
        total = start(cols)
        if unrolled:
            for i in range(tiles):
                total = scores(i, total, cols, i // per >= always)
        else:
            total = lax.fori_loop(0, tiles, functools.partial(scores, cols=cols, masked=True), total)
        inverse.append(1.0 / total)
    value_t = v_two[:, 0:HD].T
    for cols, one_over in zip(bands, inverse):
        mixed = nn(value_t, e_all[:, cols])
        outs.append(jnp.where(row_ok[:, cols], mixed * one_over, 0.0).astype(bf16))
    inverse = jnp.concatenate(inverse, axis=1)
    out = jnp.concatenate(outs, axis=1)
    ho_ref[:, 0:HD] = out[:, 0:tokens].T
    ho_ref[:, HD : 2 * HD] = out[:, tokens:wide].T

    delta = jnp.sum(grad.astype(f32) * out.astype(f32), axis=0, keepdims=True)
    high = delta.astype(bf16)
    rest = delta - high.astype(f32)
    middle = rest.astype(bf16)
    low = (rest - middle.astype(f32)).astype(bf16)
    below = lax.broadcasted_iota(jnp.int32, (HD, wide), 0)
    parts = [jnp.where(below == n, part.astype(f32), 0.0) for n, part in enumerate((high, middle, low))]
    grad_more = jnp.concatenate([grad, (-(parts[0] + parts[1] + parts[2])).astype(bf16)], axis=0)
    grad_two = (grad.astype(f32) * inverse).astype(bf16).T
    scaled = inverse * qscale

    def back(i, carry):
        at = pl.ds(i * deep, deep)
        slope = nn(v_two[at, :], grad_more)
        dscore = ((c_all[at, :] * scaled) * slope).astype(bf16)
        dkey = nn(dscore, q_two[...]).astype(bf16).reshape(deep // BLOCK, BLOCK, HD)
        dvalue = nn(e_all[at, :], grad_two).astype(bf16).reshape(deep // BLOCK, BLOCK, HD)
        at = pl.ds(i * (deep // BLOCK), deep // BLOCK)
        ga_ref[at] = jnp.where(odd == 0, dkey, dvalue)
        gb_ref[at] = jnp.where(odd == 0, dvalue, dkey)
        return carry

    if unrolled:
        for i in range(span // deep):
            back(i, 0)
    else:
        lax.fori_loop(0, span // deep, back, 0)


def sum_body(which, slots, start, last, meta, lists, counts, *refs):
    given = refs[start : start + len(which)]
    out_ref = refs[start + len(which)]
    total = refs[-1] if last else out_ref
    me = meta[0]
    total[...] = refs[0][...] if start else jnp.zeros_like(total)
    for ref, k in zip(given, which):
        row = me ^ offset(k, meta[2])

        def one(s, carry, ref=ref, row=row):
            at = lists[row, s]
            total[at] += ref[s].astype(f32)
            return carry

        lax.fori_loop(0, counts[row], one, 0)
    if last:
        out_ref[...] = total[...].astype(bf16)


def join_body(order, meta, *refs):
    out_ref = refs[-1]
    width = refs[0].shape[1]
    for near, ref in zip(order, refs):
        head = (meta[3] ^ near) & (len(order) - 1)
        out_ref[:, pl.ds(pl.multiple_of(head * width, width), width)] = ref[...]


def project_body(meta, *refs):
    pieces, (weight_ref, out_ref, x_ref) = refs[:-3], refs[-3:]

    @pl.when(pl.program_id(0) == 0)
    def _():
        width = pieces[0].shape[1]
        for i, ref in enumerate(pieces):
            at = pl.multiple_of((meta[4] ^ i) * width, width) if len(pieces) > 1 else 0
            x_ref[:, pl.ds(at, width)] = ref[...]

    out_ref[...] = nn(x_ref[...], weight_ref[...])


def adam_body(parts, copies, cut, turns, grad_ref, *refs):
    state, outs = refs[0:3], refs[3:6]
    held, made, arrived, left = refs[6:10]
    rows = grad_ref.shape[1] // cut
    lines = rows * parts
    turn = lax.axis_index("mp") if turns else 2

    def bring(i, c):
        at = pl.ds(c * lines, lines)
        return pltpu.make_async_copy(state[i].at[at], held.at[i, at], arrived.at[i, c])

    def take(i, c):
        at = pl.ds(c * lines, lines)
        return pltpu.make_async_copy(made.at[i, at], outs[i].at[at], left.at[i, c])

    for c in range(cut):
        for i in range(3):
            bring(i, c).start()
    for c in range(cut):
        for i in range(3):
            bring(i, c).wait()
        for part in range(parts):
            at = pl.ds(c * rows, rows)
            source = offset(part, turn)
            grad = grad_ref[source, at].astype(f32)
            if copies <= 4:
                for copy in range(1, copies):
                    grad = grad + grad_ref[copy * parts + source, at].astype(f32)
            else:

                def add(copy, run, source=source, at=at):
                    return run + grad_ref[copy * parts + source, at].astype(f32)

                grad = lax.fori_loop(1, copies, add, grad)
            line = part % (parts // 2) * 2 + part // (parts // 2)
            at = pl.ds(c * lines + line, rows, stride=parts)
            moment = beta_one * held[1, at, :] + (1.0 - beta_one) * grad
            second = beta_two * held[2, at, :] + (1.0 - beta_two) * grad * grad
            made[1, at, :] = moment
            made[2, at, :] = second
            made[0, at, :] = held[0, at, :] - (learn_rate / bias_one) * moment / (
                jnp.sqrt(second * (1.0 / bias_two)) + adam_eps
            )
        for i in range(3):
            take(i, c).start()
    for c in range(cut):
        for i in range(3):
            take(i, c).wait()


def local(
    queries,
    keys,
    values,
    out_weight,
    out_grad,
    bank,
    moment_one,
    moment_two,
    block_list,
    block_count,
    token_count,
):
    owners = lax.axis_size("req")
    mp_size = lax.axis_size("mp")
    me = lax.axis_index("req")
    tokens = queries.shape[0]
    kv_local = keys.shape[1] // HD
    features = queries.shape[1]
    parts = 2 * kv_local
    copies = owners // parts
    rows = bank.shape[0]
    blocks = rows // BLOCK
    slots = block_list.shape[1]
    wide = 2 * tokens
    smem = pl.BlockSpec(memory_space=pltpu.SMEM)
    vmem = pl.BlockSpec(memory_space=pltpu.VMEM)
    hbm = pl.BlockSpec(memory_space=pl.ANY)

    def lines(array):
        four = array.reshape(rows, 2, kv_local, HD).transpose(0, 2, 1, 3)
        return four.reshape(rows * parts, HD)

    def unlines(array):
        four = array.reshape(rows, kv_local, 2, HD).transpose(0, 2, 1, 3)
        return four.reshape(rows, 2, kv_local * HD)

    held_mib = owners * blocks * BLOCK * HD * 2 // MIB
    turns = parts == 8 and mp_size == 2
    place = me & (parts - 1)
    turn = lax.axis_index("mp") if turns else jnp.full_like(me, 2)
    label = jnp.where(turn == 1, label_of(place, 1), label_of(place, 0)) if turns else place
    meta = jnp.stack([me, token_count[0], turn, label, lax.axis_index("mp")])

    cut = 4
    outgoing = call(
        functools.partial(split_body, parts, copies, cut, turns),
        jax.ShapeDtypeStruct((owners, rows, HD), bf16),
        limit=6,
        in_specs=[hbm],
        out_specs=hbm,
        scratch_shapes=[
            pltpu.VMEM((rows * parts, HD), f32),
            pltpu.VMEM((parts, rows, HD), bf16),
            pltpu.SemaphoreType.DMA((cut,)),
            pltpu.SemaphoreType.DMA((cut, copies)),
        ],
        name="split",
    )(pltpu.with_memory_space_constraint(lines(bank), pltpu.HBM))
    spread = lax.all_to_all(outgoing, "req", split_axis=0, concat_axis=0, tiled=True)

    partial = lax.dot_general(
        out_weight, out_grad, (((1,), (1,)), ((), ())), preferred_element_type=f32
    )
    if mp_size == 2:
        side = lax.axis_index("mp")
        theirs = lax.dynamic_slice_in_dim(partial, (1 - side) * features, features, 0)
        mine = lax.dynamic_slice_in_dim(partial, side * features, features, 0)
        head_grad = mine + lax.ppermute(theirs, "mp", [(0, 1), (1, 0)])
    else:
        head_grad = lax.psum_scatter(partial, "mp", scatter_dimension=0, tiled=True)

    piece = jax.ShapeDtypeStruct((slots, BLOCK, HD), bf16)
    def pick(which, after):
        return call(
            functools.partial(pick_body, which, slots),
            [piece] * len(which),
            limit=held_mib + len(which) * slots * BLOCK * HD * 2 // MIB + 2,
            in_specs=[smem, smem, pl.BlockSpec(memory_space=pl.ANY), vmem],
            out_specs=[vmem] * len(which),
            name="pick",
        )(meta, block_list, after, spread.reshape(owners * blocks, BLOCK, HD))

    def swap(array, k):
        if k == 0:
            return array
        pairs = []
        for i in range(owners):
            for core in range(mp_size):
                partner = i ^ (place_of(k, core) if turns else k)
                pairs.append((i * mp_size + core, partner * mp_size + core))
        return lax.ppermute(array, ("req", "mp"), pairs)

    fetched = [None] * parts

    def fetch(which, after):
        which = [k for k in which if k < parts]
        if which:
            for k, array in zip(which, pick(which, after)):
                fetched[k] = swap(array, k)

    order = (0, 1, 2, 3) if kv_local == 4 else tuple(range(kv_local))
    phases = [order[: (kv_local + 1) // 2], order[(kv_local + 1) // 2 :]]
    phases = [[k + far for k in phase for far in (0, kv_local)] for phase in phases if phase]
    fetch(phases[0], head_grad)
    for phase in phases[1:]:
        fetch(phase[:2], fetched[kv_local])

    span = slots * BLOCK
    heads = []
    returned = [None] * parts
    back = [None] * parts
    for step, near in enumerate(order):
        far = near + kv_local
        out, returned[near], returned[far] = call(
            functools.partial(head_body, near, slots),
            [jax.ShapeDtypeStruct((tokens, 2 * HD), bf16), piece, piece],
            limit=(span * (10 * wide + 8 * HD) + 8 * tokens * features) // MIB + 8,
            in_specs=[smem, smem, hbm] + [vmem] * 6,
            out_specs=[vmem] * 3,
            scratch_shapes=[
                pltpu.VMEM((wide, HD), bf16),
                pltpu.VMEM((span + tokens, 2 * HD), bf16),
                pltpu.VMEM((span + tokens, wide), bf16),
                pltpu.VMEM((span, wide), f32),
            ],
            cost=pl.CostEstimate(
                flops=10 * span * wide * HD,
                bytes_accessed=8 * span * HD,
                transcendentals=2 * span * wide,
            ),
            name="head",
        )(
            meta,
            block_count,
            heads[-1] if heads else block_count,
            queries,
            keys,
            values,
            head_grad,
            fetched[near],
            fetched[far],
        )
        heads.append(out)
        for k in (near, far):
            back[k] = swap(returned[k], k)
        if step == 0:
            for phase in phases[1:]:
                fetch(phase[2:], out)

    sums = None
    for phase in phases:
        last = phase is phases[-1]
        start = [] if sums is None else [sums]
        sums = call(
            functools.partial(sum_body, phase, slots, len(start), last),
            jax.ShapeDtypeStruct((owners * blocks, BLOCK, HD), bf16 if last else f32),
            limit=5 * held_mib + len(phase) * slots * BLOCK * HD * 2 // MIB + 2,
            in_specs=[smem] * 3 + [vmem] * (len(start) + len(phase)),
            out_specs=vmem,
            scratch_shapes=[pltpu.VMEM((owners * blocks, BLOCK, HD), f32)] if last else [],
            name="sums",
        )(meta, block_list, block_count, *start, *[back[k] for k in phase])
    grads = lax.all_to_all(
        sums.reshape(owners, rows, HD), "req", split_axis=0, concat_axis=0, tiled=True
    )

    heads_out = heads[0]
    if kv_local > 1:
        heads_out = call(
            functools.partial(join_body, order),
            jax.ShapeDtypeStruct((tokens, features), bf16),
            limit=4,
            in_specs=[smem] + [vmem] * kv_local,
            out_specs=vmem,
            name="join",
        )(meta, *heads)
    if mp_size == 2:
        both = [heads_out, lax.ppermute(heads_out, "mp", [(0, 1), (1, 0)])]
    else:
        both = [lax.all_gather(heads_out, "mp", axis=1, tiled=True)]
    inner, columns = out_weight.shape
    strip = 384 if columns % 384 == 0 else columns
    attn_out = call(
        project_body,
        jax.ShapeDtypeStruct((tokens, columns), f32),
        limit=14,
        grid=(columns // strip,),
        in_specs=[smem]
        + [pl.BlockSpec(x.shape, lambda i: (0, 0)) for x in both]
        + [pl.BlockSpec((inner, strip), lambda i: (0, i))],
        out_specs=pl.BlockSpec((tokens, strip), lambda i: (0, i)),
        scratch_shapes=[pltpu.VMEM((tokens, inner), bf16)],
        cost=pl.CostEstimate(
            flops=2 * tokens * inner * columns,
            bytes_accessed=2 * inner * columns + 4 * tokens * columns,
            transcendentals=0,
        ),
        name="project",
    )(meta, *both, out_weight)

    state_out = jax.ShapeDtypeStruct((rows * parts, HD), f32)
    bank_next, moment_next, second_next = call(
        functools.partial(adam_body, parts, copies, cut, turns),
        [state_out] * 3,
        limit=10,
        in_specs=[vmem] + [hbm] * 3,
        out_specs=[hbm] * 3,
        scratch_shapes=[
            pltpu.VMEM((3, rows * parts, HD), f32),
            pltpu.VMEM((3, rows * parts, HD), f32),
            pltpu.SemaphoreType.DMA((3, cut)),
            pltpu.SemaphoreType.DMA((3, cut)),
        ],
        name="adam",
    )(grads, *[pltpu.with_memory_space_constraint(lines(x), pltpu.HBM) for x in (bank, moment_one, moment_two)])
    return (attn_out, unlines(bank_next), unlines(moment_next), unlines(second_next))


def solution(mesh):
    return jax.shard_map(
        local,
        mesh=mesh,
        in_specs=(
            P("req", "mp"),
            P("req", "mp"),
            P("req", "mp"),
            P(None, "mp"),
            P("req", "mp"),
            P("req", None, "mp"),
            P("req", None, "mp"),
            P("req", None, "mp"),
            P(),
            P(),
            P("req"),
        ),
        out_specs=(
            P("req", "mp"),
            P("req", None, "mp"),
            P("req", None, "mp"),
            P("req", None, "mp"),
        ),
        check_vma=False,
    )
```
